32 devices in a mesh: groups: 2 (over y), expert: 16 (over z, x, core), tensor: 1.
Axes of the slice: x: 2, y: 2, z: 4, core: 2. Of those that a mesh axis runs over, the one named last changes fastest.
Arguments:
- hidden: bfloat16 [2048, 8, 1024], P(('groups', 'expert'), None, 'tensor'), parts along dimension 0, may hold values from -6 to 6
- expert_ids: int32 [2048, 8], P(('groups', 'expert')), parts along dimension 0, may hold values from 0 to 15, all different within a row; in each aligned block of 64 rows (0 to 63, 64 to 127, ...) at most 64 rows name the same one
- gate_weights: float32 [2048, 8], P(('groups', 'expert')), parts along dimension 0, may hold values from 0.05 to 1
- down_weight: bfloat16 [16, 1024, 3584], P('expert', 'tensor'), may hold values from -0.1875 to 0.1875
Outputs:
- mixed: bfloat16 [2048, 3584], P(('groups', 'expert'), 'tensor'), parts along dimension 0
The draws below stay inside these ranges and needn't reach their ends.
There are 2 independent parts, one for each index of `groups`. The reference program is written for one: setup_inputs(seed, part) draws one part's arguments, and reference() takes and returns one part's arrays. A program takes and returns all parts, laid end to end along the dimension named above; an argument that names none is the same for every part. Nothing has to cross between parts.
Inputs may be any that keep to these rules, and one draw needn't show every extreme that they name: `expert_ids`: each row names 8 different experts. Of the 64 tokens of one index of expert, at most 64 name any one expert, and in every draw some expert is named by exactly 64 tokens of some index.
All inputs are finite; a program needn't handle non-finite values.
Results may differ from the reference program's by a relative error of at most 0.0059.
Values may be sent and summed in bfloat16 or wider, within the bound.
No kernel may reach another device: no remote copies, remote signals or barrier semaphores. Data moves between devices by JAX's collectives and lax.ppermute only.
A program may use at most 64 MiB of HBM per device.

```python
import math
import jax
import jax.numpy as jnp
import numpy as np
from jax import lax

D = 3584
FF = 1024
TOP = 8
TOK_DEV = 64
EXPERTS = 16
TOKENS = 1024
CAP = 64
FF_DEV = 1024
N_EXPERT = 16
N_TENSOR = 1


def levels(stream_key, shape, split, low, largest):
    gain, own = 1.0, jax.random.fold_in(stream_key, 6)
    for dim, shards_of in split:
        draws = jnp.exp(jax.random.uniform(jax.random.fold_in(own, dim), (shards_of,), jnp.float32, low / len(split), largest / len(split)))
        gain = gain * jnp.repeat(draws, shape[dim] // shards_of).reshape([-1 if axis == dim else 1 for axis in range(len(shape))])
    return gain


def assign_block(key, own, number, rows, amount, top, bound, skew):
    sequence = jax.random.permutation(key, amount)
    crowded, common = portions_of(amount, rows * top, bound, skew, True), portions_of(amount, rows * top, bound, skew, False)
    places = jnp.arange(amount)

    def named(lengths, offset_by):
        used = int((lengths > 0).sum())
        fixed = max(1, used // 4)
        passed = fixed + (places - fixed + offset_by * (used - fixed)) % max(1, amount - fixed)
        return jnp.zeros((amount,), jnp.int32).at[sequence[jnp.where(places < fixed, places, passed)]].set(jnp.asarray(lengths, jnp.int32))

    lengths = jnp.where(number % 4 == 0, named(crowded, number // 4), named(common, number - number // 4 - 1))
    mixed = jax.random.permutation(jax.random.fold_in(own, 3), amount)
    source_of, taker = mixed[0:amount // 2 * 2:2], mixed[1:amount // 2 * 2:2]
    margin = jnp.minimum(lengths[source_of] - 1, bound - lengths[taker]) // 2
    margin = jnp.where((source_of == sequence[0]) | (taker == sequence[0]) | (lengths[taker] == 0), 0, jnp.maximum(margin, 0))
    passed = jax.random.randint(jax.random.fold_in(own, 4), (amount // 2,), 0, 1 << 20) % (margin + 1)
    lengths = lengths.at[source_of].add(-passed).at[taker].add(passed)
    items = jnp.searchsorted(jnp.cumsum(lengths), jnp.arange(rows * top), side="right").astype(jnp.int32)
    listing = items.reshape(top, rows).T
    listing = listing[jax.random.permutation(jax.random.fold_in(own, 1), rows)]
    offset_by = jax.random.randint(jax.random.fold_in(own, 2), (rows, 1), 0, top)
    return jnp.take_along_axis(listing, (jnp.arange(top)[None, :] + offset_by) % top, axis=1)


def portions_of(amount, total, bound, slope, full):
    loads = [(1 << 20) // math.isqrt(standing ** slope) + 1 for standing in range(1, amount + 1)]
    largest = bound if full else min(bound, max(-(-total // amount), total * loads[0] // sum(loads)))
    least = 1 if total - largest >= amount - 1 else 0
    given, spare = [largest] + [least] * (amount - 1), total - largest - least * (amount - 1)
    while spare > 0:
        movable = [i for i in range(1, amount) if given[i] < largest] or [i for i in range(1, amount) if given[i] < bound]
        mass, left = sum([loads[i] for i in movable]), spare
        for i in movable:
            addition = min(bound - given[i], max(1, left * loads[i] // mass), spare)
            given[i] = given[i] + addition
            spare = spare - addition
    return np.array(given)


def scatter_about(stream_key, extent, width, bound, cuts=(), kind=jnp.bfloat16):
    result = jax.random.normal(stream_key, extent, jnp.float32) * width
    if len(cuts) > 0:
        result = levels(stream_key, extent, cuts, -0.22, 0.18) * result
    return jnp.clip(result, min=-bound, max=bound).astype(kind)


def setup_inputs(seed: int = 0, part: int = 0) -> dict:
    arg_keys = jax.random.split(jax.random.key(seed), 5)
    part_keys = jax.random.split(jax.random.fold_in(arg_keys[4], part), 5)
    hidden = scatter_about(part_keys[0], (TOKENS, TOP, FF), 1.0, 6.0, ((0, 16),))
    expert_ids_keys = jax.random.split(jax.random.fold_in(part_keys[1], 1), TOKENS // TOK_DEV)
    expert_ids_turns = jax.random.permutation(jax.random.fold_in(part_keys[1], 3), TOKENS // TOK_DEV)
    expert_ids = jax.vmap(lambda own, number: assign_block(jax.random.fold_in(part_keys[1], 2), own, number, TOK_DEV, EXPERTS, TOP, CAP, 2))(expert_ids_keys, expert_ids_turns).reshape((TOKENS, TOP))
    gate_weights = jnp.clip(jnp.exp(math.log(1.0) - 2.9957323 * jax.random.uniform(part_keys[2], (TOKENS, TOP), jnp.float32) ** levels(part_keys[2], (TOKENS, TOP), ((0, 16),), -0.2, 0.2)), 0.05, 1.0)
    down_weight = scatter_about(arg_keys[3], (EXPERTS, FF, D), FF ** -0.5, 0.1875, ((0, 16),))
    return {"hidden": hidden, "expert_ids": expert_ids, "gate_weights": gate_weights, "down_weight": down_weight}


def reference(hidden, expert_ids, gate_weights, down_weight):
    flat_ids = expert_ids.reshape(-1).astype(jnp.int32)
    flat_gates = gate_weights.reshape(-1).astype(jnp.float32)
    flat_rows = hidden.reshape(TOKENS * TOP, FF)
    arranged = jnp.argsort(flat_ids, stable=True).astype(jnp.int32)
    longest = N_EXPERT * CAP
    padded = jnp.concatenate([arranged, jnp.zeros((longest,), jnp.int32)])
    matches = (flat_ids[:, None] == jnp.arange(EXPERTS, dtype=jnp.int32)[None, :]).astype(jnp.int32)
    counts = jnp.sum(matches, axis=0).astype(jnp.int32)
    starts = (jnp.cumsum(counts) - counts).astype(jnp.int32)

    def add_expert(expert, totals):
        picks = lax.dynamic_slice(padded, (starts[expert],), (longest,)).astype(jnp.int32)
        usable = jnp.arange(longest, dtype=jnp.int32) < counts[expert]
        copy_rows = flat_rows[picks].astype(jnp.float32)
        weights = down_weight[expert].astype(jnp.float32)
        summed = jnp.zeros((longest, D), jnp.float32)
        for block in range(N_TENSOR):
            lower = block * FF_DEV
            partial_sum = jnp.dot(copy_rows[:, lower:lower + FF_DEV], weights[lower:lower + FF_DEV], preferred_element_type=jnp.float32)
            rounded = lax.optimization_barrier(partial_sum.astype(jnp.bfloat16))
            summed = summed + rounded.astype(jnp.float32)
        summed = lax.optimization_barrier(summed.astype(jnp.bfloat16)).astype(jnp.float32)
        scaled = jnp.where(usable, flat_gates[picks], jnp.zeros((longest,), jnp.float32))
        return totals.at[picks // TOP].add(scaled[:, None] * summed)

    totals = lax.fori_loop(0, EXPERTS, add_expert, jnp.zeros((TOKENS, D), jnp.float32))
    return totals.astype(jnp.bfloat16)
```

```python
import jax
import jax.numpy as jnp
from jax import lax
from jax.sharding import PartitionSpec as P


def passed_along(block, axis, distance):
    devices = range(lax.axis_size(axis))
    route = [((i - distance) % len(devices), i) for i in devices]
    return lax.ppermute(block, axis, route)


def project(arrived, weights):
    return jnp.einsum("secf,efd->secd", arrived, weights, preferred_element_type=jnp.float32)


def slotted_body(hidden, expert_ids, gate_weights, down_weight):
    token_count, choose_count, half_hidden = hidden.shape
    local_experts = down_weight.shape[0]
    owner_count = lax.axis_size("expert")
    tensor_count = lax.axis_size("tensor")
    all_experts = owner_count * local_experts
    capacity = min(token_count, max(2, 2 * token_count * choose_count // all_experts))
    flat_ids = expert_ids.reshape(-1)
    onehot = (flat_ids[:, None] == jnp.arange(all_experts, dtype=jnp.int32)[None, :]).astype(
        jnp.int32
    )
    running = jnp.cumsum(onehot, axis=0)
    ranks = jnp.sum(onehot * running, axis=1) - 1
    slots = flat_ids * capacity + ranks
    copy_rows = hidden.reshape(token_count * choose_count, half_hidden)
    outgoing = (
        jnp.zeros((all_experts * capacity, half_hidden), hidden.dtype).at[slots].set(copy_rows)
    )
    outgoing = outgoing.reshape(owner_count, local_experts, capacity, half_hidden)
    width_total = down_weight.shape[2]
    width_half = width_total // tensor_count
    position = lax.axis_index("tensor")
    other = 1 - position
    arrived = lax.all_to_all(outgoing, "expert", split_axis=0, concat_axis=0, tiled=True)
    if tensor_count == 1:
        summed = project(arrived, down_weight).astype(jnp.bfloat16)
    else:
        partial_rows = project(arrived, down_weight).astype(jnp.bfloat16)
        outbound = lax.dynamic_slice_in_dim(partial_rows, other * width_half, width_half, 3)
        mine = lax.dynamic_slice_in_dim(partial_rows, position * width_half, width_half, 3)
        inbound = passed_along(outbound, "tensor", 1)
        summed = (mine.astype(jnp.float32) + inbound.astype(jnp.float32)).astype(jnp.bfloat16)
    returned = lax.all_to_all(summed, "expert", split_axis=0, concat_axis=0, tiled=True)
    flat_back = returned.reshape(all_experts * capacity, returned.shape[3])
    picked = (
        flat_back[slots].astype(jnp.float32).reshape(token_count, choose_count, returned.shape[3])
    )
    combined = jnp.sum(picked * gate_weights[:, :, None], axis=1)
    return combined.astype(jnp.bfloat16)


def spread_rows(hidden, expert_ids, gate_weights, all_experts):
    token_count, choose_count, width = hidden.shape
    chosen = expert_ids[:, :, None] == jnp.arange(all_experts, dtype=jnp.int32)
    gates = jnp.sum(jnp.where(chosen, gate_weights[:, :, None], 0.0), axis=1).T
    same = jnp.eye(token_count, dtype=jnp.bool_)
    pick = (chosen.transpose(2, 0, 1)[:, :, None, :] & same[None, :, :, None]).astype(hidden.dtype)
    rows = jnp.dot(
        pick.reshape(all_experts * token_count, token_count * choose_count),
        hidden.reshape(token_count * choose_count, width),
        preferred_element_type=jnp.float32,
    ).reshape(all_experts, token_count, width)
    return (rows * gates[:, :, None]).astype(hidden.dtype)


def dense_body(hidden, expert_ids, gate_weights, down_weight):
    owner_count = lax.axis_size("expert")
    local_experts = down_weight.shape[0]
    token_count, _, width = hidden.shape
    outgoing = spread_rows(hidden, expert_ids, gate_weights, owner_count * local_experts)
    outgoing = outgoing.reshape(owner_count, local_experts, token_count, width)
    arrived = lax.all_to_all(outgoing, "expert", split_axis=0, concat_axis=0, tiled=True)
    mixed = jnp.einsum(
        "setf,efd->std", arrived, down_weight, preferred_element_type=jnp.float32
    ).astype(jnp.bfloat16)
    mixed = mixed.reshape(owner_count * token_count, down_weight.shape[2])
    return lax.psum_scatter(mixed, "expert", scatter_dimension=0, tiled=True)


def solution(mesh):
    placed = (
        P(("groups", "expert"), None, "tensor"),
        P(("groups", "expert"), None),
        P(("groups", "expert"), None),
        P("expert", "tensor", None),
    )

    def whole(hidden, expert_ids, gate_weights, down_weight):
        owners = mesh.shape["expert"]
        tokens = hidden.shape[0] // (mesh.shape["groups"] * owners)
        capacity = 2 * tokens * hidden.shape[1] // down_weight.shape[0]
        dense = capacity >= tokens and mesh.shape["tensor"] == 1
        return jax.shard_map(
            dense_body if dense else slotted_body,
            mesh=mesh,
            in_specs=placed,
            out_specs=P(("groups", "expert"), "tensor"),
            check_vma=False,
        )(hidden, expert_ids, gate_weights, down_weight)

    return whole
```

```python
import jax
import jax.numpy as jnp
from jax import lax
from jax.experimental import pallas as pl
from jax.experimental.pallas import tpu as pltpu
from jax.sharding import Mesh, PartitionSpec as P

CHIPS = 8
CHUNKS = 4
TILE = 896


def passed_along(block, axis, distance):
    devices = range(lax.axis_size(axis))
    route = [((i - distance) % len(devices), i) for i in devices]
    return lax.ppermute(block, axis, route)


def project(arrived, weights):
    return jnp.einsum("secf,efd->secd", arrived, weights, preferred_element_type=jnp.float32)


def slotted_body(hidden, expert_ids, gate_weights, down_weight):
    token_count, choose_count, half_hidden = hidden.shape
    local_experts = down_weight.shape[0]
    owner_count = lax.axis_size("expert")
    tensor_count = lax.axis_size("tensor")
    all_experts = owner_count * local_experts
    capacity = min(token_count, max(2, 2 * token_count * choose_count // all_experts))
    flat_ids = expert_ids.reshape(-1)
    onehot = (flat_ids[:, None] == jnp.arange(all_experts, dtype=jnp.int32)[None, :]).astype(
        jnp.int32
    )
    running = jnp.cumsum(onehot, axis=0)
    ranks = jnp.sum(onehot * running, axis=1) - 1
    slots = flat_ids * capacity + ranks
    copy_rows = hidden.reshape(token_count * choose_count, half_hidden)
    outgoing = (
        jnp.zeros((all_experts * capacity, half_hidden), hidden.dtype).at[slots].set(copy_rows)
    )
    outgoing = outgoing.reshape(owner_count, local_experts, capacity, half_hidden)
    width_total = down_weight.shape[2]
    width_half = width_total // tensor_count
    position = lax.axis_index("tensor")
    other = 1 - position
    arrived = lax.all_to_all(outgoing, "expert", split_axis=0, concat_axis=0, tiled=True)
    if tensor_count == 1:
        summed = project(arrived, down_weight).astype(jnp.bfloat16)
    else:
        partial_rows = project(arrived, down_weight).astype(jnp.bfloat16)
        outbound = lax.dynamic_slice_in_dim(partial_rows, other * width_half, width_half, 3)
        mine = lax.dynamic_slice_in_dim(partial_rows, position * width_half, width_half, 3)
        inbound = passed_along(outbound, "tensor", 1)
        summed = (mine.astype(jnp.float32) + inbound.astype(jnp.float32)).astype(jnp.bfloat16)
    returned = lax.all_to_all(summed, "expert", split_axis=0, concat_axis=0, tiled=True)
    flat_back = returned.reshape(all_experts * capacity, returned.shape[3])
    picked = (
        flat_back[slots].astype(jnp.float32).reshape(token_count, choose_count, returned.shape[3])
    )
    combined = jnp.sum(picked * gate_weights[:, :, None], axis=1)
    return combined.astype(jnp.bfloat16)


def spread_kernel(own_ref, flat_ids_ref, ids_ref, gates_ref, hidden_ref, *out_refs):
    token_count, choose_count = ids_ref.shape
    own = own_ref[0]
    shape = (token_count, token_count * choose_count)
    row = lax.broadcasted_iota(jnp.int32, shape, 0) * choose_count
    column = lax.broadcasted_iota(jnp.int32, shape, 1)
    same = (column >= row) & (column < row + choose_count)
    own_row = jnp.where(same, flat_ids_ref[...], -1)
    for relative, out_ref in enumerate(out_refs):
        for core in range(2):
            expert = own ^ (2 * relative + core)
            pick = (own_row == expert).astype(jnp.float32).astype(hidden_ref.dtype)
            gate = jnp.sum(
                jnp.where(ids_ref[...] == expert, gates_ref[...], 0.0), axis=1, keepdims=True
            )
            rows = jnp.dot(pick, hidden_ref[...], preferred_element_type=jnp.float32)
            out_ref[core] = (rows * gate).astype(out_ref.dtype)


def spread_rows(hidden, expert_ids, gate_weights, own):
    token_count, choose_count, width = hidden.shape
    vmem = pl.BlockSpec(memory_space=pltpu.VMEM)
    block = jax.ShapeDtypeStruct((2, token_count, width), hidden.dtype)
    return pl.pallas_call(
        spread_kernel,
        in_specs=[pl.BlockSpec(memory_space=pltpu.SMEM)] + [vmem] * 4,
        out_specs=[vmem] * CHIPS,
        out_shape=[block] * CHIPS,
        compiler_params=pltpu.CompilerParams(vmem_limit_bytes=32 << 20),
        name="spread_rows",
    )(
        own.reshape(1),
        expert_ids.reshape(1, token_count * choose_count),
        expert_ids,
        gate_weights,
        hidden.reshape(token_count * choose_count, width),
    )


def mix_kernel(*refs):
    rows, (near_ref, far_ref, out_ref) = refs[:-3], refs[-3:]
    tokens = rows[0].shape[1]
    near = jnp.concatenate([ref[0] for ref in rows], axis=0)
    far = jnp.concatenate([ref[1] for ref in rows], axis=0)
    total = jnp.dot(near, near_ref[...], preferred_element_type=jnp.float32)
    total += jnp.dot(far, far_ref[...], preferred_element_type=jnp.float32)
    out_ref[...] = total.reshape(len(rows), tokens, -1).astype(out_ref.dtype)


def mix(rows, near, far, start, width, tile):
    _, tokens, depth = rows[0].shape
    whole = pl.BlockSpec((2, tokens, depth), lambda i: (0, 0, 0))
    weight = pl.BlockSpec((depth, tile), lambda i: (0, start // tile + i))
    return pl.pallas_call(
        mix_kernel,
        grid=(width // tile,),
        in_specs=[whole] * len(rows) + [weight] * 2,
        out_specs=pl.BlockSpec((len(rows), tokens, tile), lambda i: (0, 0, i)),
        out_shape=jax.ShapeDtypeStruct((len(rows), tokens, width), jnp.bfloat16),
        compiler_params=pltpu.CompilerParams(vmem_limit_bytes=32 << 20),
        cost_estimate=pl.CostEstimate(
            flops=4 * len(rows) * tokens * depth * width,
            bytes_accessed=4 * depth * width + 2 * len(rows) * tokens * (2 * depth + width),
            transcendentals=0,
        ),
        name="mix",
    )(*rows, near, far)


def swap(block, axis, distance):
    return lax.ppermute(block, axis, [(i, i ^ distance) for i in range(lax.axis_size(axis))])


def send_to_chip(block, relative):
    sizes = (lax.axis_size("z"), lax.axis_size("x"))
    return lax.ppermute(
        block, ("z", "x"), [(i, i ^ relative) for i in range(sizes[0] * sizes[1])]
    )


def dense_body(hidden, expert_ids, gate_weights, down_weight):
    width_total = down_weight.shape[2]
    own = (lax.axis_index("z") * 2 + lax.axis_index("x")) * 2 + lax.axis_index("core")
    near = down_weight[0]
    far = swap(near, "core", 1)
    outgoing = spread_rows(hidden, expert_ids, gate_weights, own)
    arrived = [outgoing[0]] + [send_to_chip(outgoing[r], r) for r in range(1, CHIPS)]
    chunk = width_total // CHUNKS
    results = []
    for start in range(0, width_total, chunk):
        given = mix(arrived[1::2], near, far, start, chunk, TILE)
        kept = mix(arrived[0::2], near, far, start, chunk, TILE)
        taken = swap(given, "x", 1)
        line = kept.astype(jnp.float32) + taken.astype(jnp.float32)
        pair = line[0::2] + swap(line[1::2].astype(jnp.bfloat16), "z", 1).astype(jnp.float32)
        last = pair[0] + swap(pair[1].astype(jnp.bfloat16), "z", 2).astype(jnp.float32)
        results.append(last.astype(jnp.bfloat16))
    return jnp.concatenate(results, axis=1)


def solution(mesh):
    groups, owners, tensors = (mesh.shape[axis] for axis in ("groups", "expert", "tensor"))

    def whole(hidden, expert_ids, gate_weights, down_weight):
        tokens = hidden.shape[0] // (groups * owners)
        capacity = 2 * tokens * hidden.shape[1] // down_weight.shape[0]
        one_each = owners == 2 * CHIPS and down_weight.shape[0] == owners
        if tensors == 1 and one_each and capacity >= tokens:
            axes = ("groups", "z", "x", "core")
            used = Mesh(mesh.devices.reshape(groups, CHIPS // 2, 2, 2), axes)
            run, batch = dense_body, P(axes)
            weight, out = P(axes[1:]), P(axes)
        else:
            used, run, batch = mesh, slotted_body, P(("groups", "expert"))
            weight = P("expert", "tensor", None)
            out = P(("groups", "expert"), "tensor")
        rows = batch if tensors == 1 else P(("groups", "expert"), None, "tensor")
        return jax.shard_map(
            run,
            mesh=used,
            in_specs=(rows, batch, batch, weight),
            out_specs=out,
            check_vma=False,
        )(hidden, expert_ids, gate_weights, down_weight)

    return whole
```

```python
import functools

import jax
import jax.numpy as jnp
from jax import lax
from jax.experimental import pallas as pl
from jax.experimental.pallas import tpu as pltpu
from jax.sharding import Mesh, PartitionSpec as P

CHIPS = 8
CHUNKS = 4


def passed_along(block, axis, distance):
    devices = range(lax.axis_size(axis))
    route = [((i - distance) % len(devices), i) for i in devices]
    return lax.ppermute(block, axis, route)


def project(arrived, weights):
    return jnp.einsum("secf,efd->secd", arrived, weights, preferred_element_type=jnp.float32)


def slotted_body(hidden, expert_ids, gate_weights, down_weight):
    token_count, choose_count, half_hidden = hidden.shape
    local_experts = down_weight.shape[0]
    owner_count = lax.axis_size("expert")
    tensor_count = lax.axis_size("tensor")
    all_experts = owner_count * local_experts
    capacity = min(token_count, max(2, 2 * token_count * choose_count // all_experts))
    flat_ids = expert_ids.reshape(-1)
    onehot = (flat_ids[:, None] == jnp.arange(all_experts, dtype=jnp.int32)[None, :]).astype(
        jnp.int32
    )
    running = jnp.cumsum(onehot, axis=0)
    ranks = jnp.sum(onehot * running, axis=1) - 1
    slots = flat_ids * capacity + ranks
    copy_rows = hidden.reshape(token_count * choose_count, half_hidden)
    outgoing = (
        jnp.zeros((all_experts * capacity, half_hidden), hidden.dtype).at[slots].set(copy_rows)
    )
    outgoing = outgoing.reshape(owner_count, local_experts, capacity, half_hidden)
    width_total = down_weight.shape[2]
    width_half = width_total // tensor_count
    position = lax.axis_index("tensor")
    other = 1 - position
    arrived = lax.all_to_all(outgoing, "expert", split_axis=0, concat_axis=0, tiled=True)
    if tensor_count == 1:
        summed = project(arrived, down_weight).astype(jnp.bfloat16)
    else:
        partial_rows = project(arrived, down_weight).astype(jnp.bfloat16)
        outbound = lax.dynamic_slice_in_dim(partial_rows, other * width_half, width_half, 3)
        mine = lax.dynamic_slice_in_dim(partial_rows, position * width_half, width_half, 3)
        inbound = passed_along(outbound, "tensor", 1)
        summed = (mine.astype(jnp.float32) + inbound.astype(jnp.float32)).astype(jnp.bfloat16)
    returned = lax.all_to_all(summed, "expert", split_axis=0, concat_axis=0, tiled=True)
    flat_back = returned.reshape(all_experts * capacity, returned.shape[3])
    picked = (
        flat_back[slots].astype(jnp.float32).reshape(token_count, choose_count, returned.shape[3])
    )
    combined = jnp.sum(picked * gate_weights[:, :, None], axis=1)
    return combined.astype(jnp.bfloat16)


def spread_kernel(relatives, own_ref, ids_ref, gates_ref, hidden_ref, *refs):
    out_refs = refs[-len(relatives) :]
    own = own_ref[0]
    choose_count, token_count = ids_ref.shape
    shape = (token_count, token_count * choose_count)
    row = lax.broadcasted_iota(jnp.int32, shape, 0) * choose_count
    column = lax.broadcasted_iota(jnp.int32, shape, 1)
    same = (column >= row) & (column < row + choose_count)
    across = (choose_count, token_count * choose_count)
    choice = lax.rem(lax.broadcasted_iota(jnp.int32, across, 1), choose_count)
    repeat = (choice == lax.broadcasted_iota(jnp.int32, across, 0)).astype(jnp.float32)
    ids, gate_weights = ids_ref[...].T, gates_ref[...].T
    spread_ids = jnp.dot(ids.astype(jnp.float32), repeat, preferred_element_type=jnp.float32)
    own_row = jnp.where(same, (spread_ids + 0.5).astype(jnp.int32), -1)
    for at in range(0, len(relatives), 2):
        picks, gates = [], []
        for relative in relatives[at : at + 2]:
            for core in range(2):
                expert = own ^ (2 * relative + core)
                picks.append((own_row == expert).astype(jnp.float32).astype(hidden_ref.dtype))
                gates.append(
                    jnp.sum(jnp.where(ids == expert, gate_weights, 0.0), axis=1, keepdims=True)
                )
        rows = jnp.dot(
            jnp.concatenate(picks, axis=0), hidden_ref[...], preferred_element_type=jnp.float32
        )
        scaled = (rows * jnp.concatenate(gates, axis=0)).astype(hidden_ref.dtype)
        for place in range(len(picks) // 2):
            block = scaled[2 * place * token_count : 2 * (place + 1) * token_count]
            out_refs[at + place][...] = block.reshape(2, token_count, -1)


def spread_rows(hidden, expert_ids, gate_weights, own, relatives, held=None):
    token_count, choose_count, width = hidden.shape
    vmem = pl.BlockSpec(memory_space=pltpu.VMEM)
    block = jax.ShapeDtypeStruct((2, token_count, width), hidden.dtype)
    more = [] if held is None else [held]
    return pl.pallas_call(
        functools.partial(spread_kernel, relatives),
        in_specs=[pl.BlockSpec(memory_space=pltpu.SMEM)] + [vmem] * (3 + len(more)),
        out_specs=[vmem] * len(relatives),
        out_shape=[block] * len(relatives),
        compiler_params=pltpu.CompilerParams(vmem_limit_bytes=24 << 20),
        name="spread_rows",
    )(
        own.reshape(1),
        expert_ids.T,
        gate_weights.T,
        hidden.reshape(token_count * choose_count, width),
        *more,
    )


def mix_kernel(start, *refs):
    rows, (near_ref, far_ref, out_ref) = refs[:-3], refs[-3:]
    tokens, width = rows[0].shape[1], out_ref.shape[2]
    columns = pl.ds(start, width)
    near = jnp.concatenate([ref[0] for ref in rows], axis=0)
    far = jnp.concatenate([ref[1] for ref in rows], axis=0)
    total = jnp.dot(near, near_ref[:, columns], preferred_element_type=jnp.float32)
    total += jnp.dot(far, far_ref[:, columns], preferred_element_type=jnp.float32)
    out_ref[...] = total.reshape(len(rows), tokens, -1).astype(out_ref.dtype)


def mix(rows, near, far, start, width):
    _, tokens, depth = rows[0].shape
    vmem = pl.BlockSpec(memory_space=pltpu.VMEM)
    return pl.pallas_call(
        functools.partial(mix_kernel, start),
        in_specs=[vmem] * (len(rows) + 2),
        out_specs=vmem,
        out_shape=jax.ShapeDtypeStruct((len(rows), tokens, width), jnp.bfloat16),
        compiler_params=pltpu.CompilerParams(vmem_limit_bytes=24 << 20),
        cost_estimate=pl.CostEstimate(
            flops=4 * len(rows) * tokens * depth * width,
            bytes_accessed=2 * len(rows) * tokens * (2 * depth + width),
            transcendentals=0,
        ),
        name="mix",
    )(*rows, near, far)


def swap(block, axis, distance):
    return lax.ppermute(block, axis, [(i, i ^ distance) for i in range(lax.axis_size(axis))])


def send_to_chip(block, relative):
    sizes = (lax.axis_size("z"), lax.axis_size("x"))
    return lax.ppermute(
        block, ("z", "x"), [(i, i ^ relative) for i in range(sizes[0] * sizes[1])]
    )


def dense_body(hidden, expert_ids, gate_weights, down_weight):
    width_total = down_weight.shape[2]
    own = (lax.axis_index("z") * 2 + lax.axis_index("x")) * 2 + lax.axis_index("core")
    near = down_weight[0]
    far = swap(near, "core", 1)
    odd, even = (7, 5, 3, 1), (6, 4, 2, 0)
    arrived = [None] * CHIPS
    blocks = spread_rows(hidden, expert_ids, gate_weights, own, odd)
    for relative, block in zip(odd, blocks):
        arrived[relative] = send_to_chip(block, relative)
    blocks = spread_rows(hidden, expert_ids, gate_weights, own, even, near)
    for relative, block in zip(even, blocks):
        arrived[relative] = send_to_chip(block, relative) if relative else block
    chunk = width_total // CHUNKS
    results = []
    for start in range(0, width_total, chunk):
        given = mix(arrived[1::2], near, far, start, chunk)
        kept = mix(arrived[0::2], near, far, start, chunk)
        taken = swap(given, "x", 1)
        line = kept.astype(jnp.float32) + taken.astype(jnp.float32)
        pair = line[0::2] + swap(line[1::2].astype(jnp.bfloat16), "z", 1).astype(jnp.float32)
        last = pair[0] + swap(pair[1].astype(jnp.bfloat16), "z", 2).astype(jnp.float32)
        results.append(last.astype(jnp.bfloat16))
    return jnp.concatenate(results, axis=1)


def solution(mesh):
    groups, owners, tensors = (mesh.shape[axis] for axis in ("groups", "expert", "tensor"))

    def whole(hidden, expert_ids, gate_weights, down_weight):
        tokens = hidden.shape[0] // (groups * owners)
        capacity = 2 * tokens * hidden.shape[1] // down_weight.shape[0]
        one_each = owners == 2 * CHIPS and down_weight.shape[0] == owners
        if tensors == 1 and one_each and capacity >= tokens:
            axes = ("groups", "z", "x", "core")
            used = Mesh(mesh.devices.reshape(groups, CHIPS // 2, 2, 2), axes)
            run, batch = dense_body, P(axes)
            weight, out = P(axes[1:]), P(axes)
        else:
            used, run, batch = mesh, slotted_body, P(("groups", "expert"))
            weight = P("expert", "tensor", None)
            out = P(("groups", "expert"), "tensor")
        rows = batch if tensors == 1 else P(("groups", "expert"), None, "tensor")
        return jax.shard_map(
            run,
            mesh=used,
            in_specs=(rows, batch, batch, weight),
            out_specs=out,
            check_vma=False,
        )(hidden, expert_ids, gate_weights, down_weight)

    return whole
```

```python
import functools

import jax
import jax.numpy as jnp
from jax import lax
from jax.experimental import pallas as pl
from jax.experimental.pallas import tpu as pltpu
from jax.sharding import Mesh, PartitionSpec as P

CHIPS = 8
TILE = 256
COLUMNS = ((0, 1024), (1024, 1024), (2048, 1024), (3072, 512))


def passed_along(block, axis, distance):
    devices = range(lax.axis_size(axis))
    route = [((i - distance) % len(devices), i) for i in devices]
    return lax.ppermute(block, axis, route)


def project(arrived, weights):
    return jnp.einsum("secf,efd->secd", arrived, weights, preferred_element_type=jnp.float32)


def slotted_body(hidden, expert_ids, gate_weights, down_weight):
    token_count, choose_count, half_hidden = hidden.shape
    local_experts = down_weight.shape[0]
    owner_count = lax.axis_size("expert")
    tensor_count = lax.axis_size("tensor")
    all_experts = owner_count * local_experts
    capacity = min(token_count, max(2, 2 * token_count * choose_count // all_experts))
    flat_ids = expert_ids.reshape(-1)
    onehot = (flat_ids[:, None] == jnp.arange(all_experts, dtype=jnp.int32)[None, :]).astype(
        jnp.int32
    )
    running = jnp.cumsum(onehot, axis=0)
    ranks = jnp.sum(onehot * running, axis=1) - 1
    slots = flat_ids * capacity + ranks
    copy_rows = hidden.reshape(token_count * choose_count, half_hidden)
    outgoing = (
        jnp.zeros((all_experts * capacity, half_hidden), hidden.dtype).at[slots].set(copy_rows)
    )
    outgoing = outgoing.reshape(owner_count, local_experts, capacity, half_hidden)
    width_total = down_weight.shape[2]
    width_half = width_total // tensor_count
    position = lax.axis_index("tensor")
    other = 1 - position
    arrived = lax.all_to_all(outgoing, "expert", split_axis=0, concat_axis=0, tiled=True)
    if tensor_count == 1:
        summed = project(arrived, down_weight).astype(jnp.bfloat16)
    else:
        partial_rows = project(arrived, down_weight).astype(jnp.bfloat16)
        outbound = lax.dynamic_slice_in_dim(partial_rows, other * width_half, width_half, 3)
        mine = lax.dynamic_slice_in_dim(partial_rows, position * width_half, width_half, 3)
        inbound = passed_along(outbound, "tensor", 1)
        summed = (mine.astype(jnp.float32) + inbound.astype(jnp.float32)).astype(jnp.bfloat16)
    returned = lax.all_to_all(summed, "expert", split_axis=0, concat_axis=0, tiled=True)
    flat_back = returned.reshape(all_experts * capacity, returned.shape[3])
    picked = (
        flat_back[slots].astype(jnp.float32).reshape(token_count, choose_count, returned.shape[3])
    )
    combined = jnp.sum(picked * gate_weights[:, :, None], axis=1)
    return combined.astype(jnp.bfloat16)


def spread_kernel(relatives, own_ref, ids_ref, gates_ref, hidden_ref, *refs):
    out_refs = refs[-len(relatives) :]
    own = own_ref[0]
    choose_count, token_count = ids_ref.shape
    shape = (token_count, token_count * choose_count)
    row = lax.broadcasted_iota(jnp.int32, shape, 0) * choose_count
    column = lax.broadcasted_iota(jnp.int32, shape, 1)
    same = (column >= row) & (column < row + choose_count)
    across = (choose_count, token_count * choose_count)
    choice = lax.rem(lax.broadcasted_iota(jnp.int32, across, 1), choose_count)
    repeat = (choice == lax.broadcasted_iota(jnp.int32, across, 0)).astype(jnp.float32)
    ids, gate_weights = ids_ref[...].T, gates_ref[...].T
    spread_ids = jnp.dot(ids.astype(jnp.float32), repeat, preferred_element_type=jnp.float32)
    own_row = jnp.where(same, (spread_ids + 0.5).astype(jnp.int32), -1)
    for at in range(0, len(relatives), 2):
        picks, gates = [], []
        for relative in relatives[at : at + 2]:
            for core in range(2):
                expert = own ^ (2 * relative + core)
                picks.append((own_row == expert).astype(jnp.float32).astype(hidden_ref.dtype))
                gates.append(
                    jnp.sum(jnp.where(ids == expert, gate_weights, 0.0), axis=1, keepdims=True)
                )
        rows = jnp.dot(
            jnp.concatenate(picks, axis=0), hidden_ref[...], preferred_element_type=jnp.float32
        )
        scaled = (rows * jnp.concatenate(gates, axis=0)).astype(hidden_ref.dtype)
        for place in range(len(picks) // 2):
            block = scaled[2 * place * token_count : 2 * (place + 1) * token_count]
            out_refs[at + place][...] = block.reshape(2, token_count, -1)


def spread_rows(hidden, expert_ids, gate_weights, own, relatives, held=None):
    token_count, choose_count, width = hidden.shape
    vmem = pl.BlockSpec(memory_space=pltpu.VMEM)
    block = jax.ShapeDtypeStruct((2, token_count, width), hidden.dtype)
    more = [] if held is None else [held]
    return pl.pallas_call(
        functools.partial(spread_kernel, relatives),
        in_specs=[pl.BlockSpec(memory_space=pltpu.SMEM)] + [vmem] * (3 + len(more)),
        out_specs=[vmem] * len(relatives),
        out_shape=[block] * len(relatives),
        compiler_params=pltpu.CompilerParams(vmem_limit_bytes=24 << 20),
        name="spread_rows",
    )(
        own.reshape(1),
        expert_ids.T,
        gate_weights.T,
        hidden.reshape(token_count * choose_count, width),
        *more,
    )


def mix_kernel(*refs):
    rows, (near_ref, far_ref, out_ref) = refs[:-3], refs[-3:]
    tokens = rows[0].shape[1]
    near = jnp.concatenate([ref[0] for ref in rows], axis=0)
    far = jnp.concatenate([ref[1] for ref in rows], axis=0)
    total = jnp.dot(near, near_ref[...], preferred_element_type=jnp.float32)
    total += jnp.dot(far, far_ref[...], preferred_element_type=jnp.float32)
    out_ref[...] = total.reshape(len(rows), tokens, -1).astype(out_ref.dtype)


def mix(rows, near, far, start, width):
    _, tokens, depth = rows[0].shape
    whole = pl.BlockSpec((2, tokens, depth), lambda i: (0, 0, 0))
    weight = pl.BlockSpec((depth, TILE), lambda i: (0, start // TILE + i))
    return pl.pallas_call(
        mix_kernel,
        grid=(width // TILE,),
        in_specs=[whole] * len(rows) + [weight] * 2,
        out_specs=pl.BlockSpec((len(rows), tokens, TILE), lambda i: (0, 0, i)),
        out_shape=jax.ShapeDtypeStruct((len(rows), tokens, width), jnp.bfloat16),
        compiler_params=pltpu.CompilerParams(vmem_limit_bytes=24 << 20),
        cost_estimate=pl.CostEstimate(
            flops=4 * len(rows) * tokens * depth * width,
            bytes_accessed=4 * depth * width + 2 * len(rows) * tokens * (2 * depth + width),
            transcendentals=0,
        ),
        name="mix",
    )(*rows, near, far)


def swap(block, axis, distance):
    return lax.ppermute(block, axis, [(i, i ^ distance) for i in range(lax.axis_size(axis))])


def send_to_chip(block, relative):
    sizes = (lax.axis_size("z"), lax.axis_size("x"))
    return lax.ppermute(
        block, ("z", "x"), [(i, i ^ relative) for i in range(sizes[0] * sizes[1])]
    )


def dense_body(hidden, expert_ids, gate_weights, down_weight):
    own = (lax.axis_index("z") * 2 + lax.axis_index("x")) * 2 + lax.axis_index("core")
    near = down_weight[0]
    far = swap(near, "core", 1)
    odd, even = (7, 5, 3, 1), (6, 4, 2, 0)
    arrived = [None] * CHIPS
    blocks = spread_rows(hidden, expert_ids, gate_weights, own, odd)
    for relative, block in zip(odd, blocks):
        arrived[relative] = send_to_chip(block, relative)
    blocks = spread_rows(hidden, expert_ids, gate_weights, own, even, near)
    for relative, block in zip(even, blocks):
        block, arrived[relative + 1] = lax.optimization_barrier((block, arrived[relative + 1]))
        arrived[relative] = send_to_chip(block, relative) if relative else block
    given = [mix(arrived[1::2], near, far, *columns) for columns in COLUMNS]
    taken = [swap(block, "x", 1) for block in given]
    results = []
    for at, columns in enumerate(COLUMNS):
        kept = mix(arrived[0::2], near, far, *columns)
        line = kept.astype(jnp.float32) + taken[at].astype(jnp.float32)
        half = swap(line[1::2].astype(jnp.bfloat16), "z", 1)
        if at + 1 < len(COLUMNS):
            half, taken[at + 1] = lax.optimization_barrier((half, taken[at + 1]))
        pair = line[0::2] + half.astype(jnp.float32)
        last = pair[0] + swap(pair[1].astype(jnp.bfloat16), "z", 2).astype(jnp.float32)
        results.append(last.astype(jnp.bfloat16))
    return jnp.concatenate(results, axis=1)


def solution(mesh):
    groups, owners, tensors = (mesh.shape[axis] for axis in ("groups", "expert", "tensor"))

    def whole(hidden, expert_ids, gate_weights, down_weight):
        tokens = hidden.shape[0] // (groups * owners)
        capacity = 2 * tokens * hidden.shape[1] // down_weight.shape[0]
        one_each = owners == 2 * CHIPS and down_weight.shape[0] == owners
        if tensors == 1 and one_each and capacity >= tokens:
            axes = ("groups", "z", "x", "core")
            used = Mesh(mesh.devices.reshape(groups, CHIPS // 2, 2, 2), axes)
            run, batch = dense_body, P(axes)
            weight, out = P(axes[1:]), P(axes)
        else:
            used, run, batch = mesh, slotted_body, P(("groups", "expert"))
            weight = P("expert", "tensor", None)
            out = P(("groups", "expert"), "tensor")
        rows = batch if tensors == 1 else P(("groups", "expert"), None, "tensor")
        return jax.shard_map(
            run,
            mesh=used,
            in_specs=(rows, batch, batch, weight),
            out_specs=out,
            check_vma=False,
        )(hidden, expert_ids, gate_weights, down_weight)

    return whole
```

```python
import functools

import jax
import jax.numpy as jnp
from jax import lax
from jax.experimental import pallas as pl
from jax.experimental.pallas import tpu as pltpu
from jax.sharding import Mesh, PartitionSpec as P

CHIPS = 8
TILE = 512
COLUMNS = ((0, 1024), (1024, 1024), (2048, 1024), (3072, 512))


def passed_along(block, axis, distance):
    devices = range(lax.axis_size(axis))
    route = [((i - distance) % len(devices), i) for i in devices]
    return lax.ppermute(block, axis, route)


def project(arrived, weights):
    return jnp.einsum("secf,efd->secd", arrived, weights, preferred_element_type=jnp.float32)


def slotted_body(hidden, expert_ids, gate_weights, down_weight):
    token_count, choose_count, half_hidden = hidden.shape
    local_experts = down_weight.shape[0]
    owner_count = lax.axis_size("expert")
    tensor_count = lax.axis_size("tensor")
    all_experts = owner_count * local_experts
    capacity = min(token_count, max(2, 2 * token_count * choose_count // all_experts))
    flat_ids = expert_ids.reshape(-1)
    onehot = (flat_ids[:, None] == jnp.arange(all_experts, dtype=jnp.int32)[None, :]).astype(
        jnp.int32
    )
    running = jnp.cumsum(onehot, axis=0)
    ranks = jnp.sum(onehot * running, axis=1) - 1
    slots = flat_ids * capacity + ranks
    copy_rows = hidden.reshape(token_count * choose_count, half_hidden)
    outgoing = (
        jnp.zeros((all_experts * capacity, half_hidden), hidden.dtype).at[slots].set(copy_rows)
    )
    outgoing = outgoing.reshape(owner_count, local_experts, capacity, half_hidden)
    width_total = down_weight.shape[2]
    width_half = width_total // tensor_count
    position = lax.axis_index("tensor")
    other = 1 - position
    arrived = lax.all_to_all(outgoing, "expert", split_axis=0, concat_axis=0, tiled=True)
    if tensor_count == 1:
        summed = project(arrived, down_weight).astype(jnp.bfloat16)
    else:
        partial_rows = project(arrived, down_weight).astype(jnp.bfloat16)
        outbound = lax.dynamic_slice_in_dim(partial_rows, other * width_half, width_half, 3)
        mine = lax.dynamic_slice_in_dim(partial_rows, position * width_half, width_half, 3)
        inbound = passed_along(outbound, "tensor", 1)
        summed = (mine.astype(jnp.float32) + inbound.astype(jnp.float32)).astype(jnp.bfloat16)
    returned = lax.all_to_all(summed, "expert", split_axis=0, concat_axis=0, tiled=True)
    flat_back = returned.reshape(all_experts * capacity, returned.shape[3])
    picked = (
        flat_back[slots].astype(jnp.float32).reshape(token_count, choose_count, returned.shape[3])
    )
    combined = jnp.sum(picked * gate_weights[:, :, None], axis=1)
    return combined.astype(jnp.bfloat16)


def spread_kernel(relatives, own_ref, ids_ref, gates_ref, hidden_ref, *refs):
    out_refs = refs[-len(relatives) :]
    own = own_ref[0]
    choose_count, token_count = ids_ref.shape
    shape = (token_count, token_count * choose_count)
    row = lax.broadcasted_iota(jnp.int32, shape, 0) * choose_count
    column = lax.broadcasted_iota(jnp.int32, shape, 1)
    same = (column >= row) & (column < row + choose_count)
    across = (choose_count, token_count * choose_count)
    choice = lax.rem(lax.broadcasted_iota(jnp.int32, across, 1), choose_count)
    repeat = (choice == lax.broadcasted_iota(jnp.int32, across, 0)).astype(jnp.float32)
    ids, gate_weights = ids_ref[...].T, gates_ref[...].T
    spread_ids = jnp.dot(ids.astype(jnp.float32), repeat, preferred_element_type=jnp.float32)
    own_row = jnp.where(same, (spread_ids + 0.5).astype(jnp.int32), -1)
    for at in range(0, len(relatives), 2):
        picks, gates = [], []
        for relative in relatives[at : at + 2]:
            for core in range(2):
                expert = own ^ (2 * relative + core)
                picks.append((own_row == expert).astype(jnp.float32).astype(hidden_ref.dtype))
                gates.append(
                    jnp.sum(jnp.where(ids == expert, gate_weights, 0.0), axis=1, keepdims=True)
                )
        rows = jnp.dot(
            jnp.concatenate(picks, axis=0), hidden_ref[...], preferred_element_type=jnp.float32
        )
        scaled = (rows * jnp.concatenate(gates, axis=0)).astype(hidden_ref.dtype)
        for place in range(len(picks) // 2):
            block = scaled[2 * place * token_count : 2 * (place + 1) * token_count]
            out_refs[at + place][...] = block.reshape(2, token_count, -1)


def spread_rows(hidden, expert_ids, gate_weights, own, relatives, held=None):
    token_count, choose_count, width = hidden.shape
    vmem = pl.BlockSpec(memory_space=pltpu.VMEM)
    block = jax.ShapeDtypeStruct((2, token_count, width), hidden.dtype)
    more = [] if held is None else [held]
    return pl.pallas_call(
        functools.partial(spread_kernel, relatives),
        in_specs=[pl.BlockSpec(memory_space=pltpu.SMEM)] + [vmem] * (3 + len(more)),
        out_specs=[vmem] * len(relatives),
        out_shape=[block] * len(relatives),
        compiler_params=pltpu.CompilerParams(vmem_limit_bytes=24 << 20),
        name="spread_rows",
    )(
        own.reshape(1),
        expert_ids.T,
        gate_weights.T,
        hidden.reshape(token_count * choose_count, width),
        *more,
    )


def mix_kernel(*refs):
    rows, (near_ref, far_ref, out_ref, joined_ref) = refs[:-4], refs[-4:]
    tokens = rows[0].shape[1]

    @pl.when(pl.program_id(0) == 0)
    def _():
        for place, ref in enumerate(rows):
            joined_ref[:, place * tokens : (place + 1) * tokens] = ref[...]

    total = jnp.dot(joined_ref[0], near_ref[...], preferred_element_type=jnp.float32)
    total += jnp.dot(joined_ref[1], far_ref[...], preferred_element_type=jnp.float32)
    out_ref[...] = total.reshape(len(rows), tokens, -1).astype(out_ref.dtype)


def mix(rows, near, far, start, width):
    _, tokens, depth = rows[0].shape
    whole = pl.BlockSpec((2, tokens, depth), lambda i: (0, 0, 0))
    weight = pl.BlockSpec((depth, TILE), lambda i: (0, start // TILE + i))
    return pl.pallas_call(
        mix_kernel,
        grid=(width // TILE,),
        in_specs=[whole] * len(rows) + [weight] * 2,
        out_specs=pl.BlockSpec((len(rows), tokens, TILE), lambda i: (0, 0, i)),
        out_shape=jax.ShapeDtypeStruct((len(rows), tokens, width), jnp.bfloat16),
        scratch_shapes=[pltpu.VMEM((2, len(rows) * tokens, depth), jnp.bfloat16)],
        compiler_params=pltpu.CompilerParams(vmem_limit_bytes=24 << 20),
        cost_estimate=pl.CostEstimate(
            flops=4 * len(rows) * tokens * depth * width,
            bytes_accessed=4 * depth * width + 2 * len(rows) * tokens * (2 * depth + width),
            transcendentals=0,
        ),
        name="mix",
    )(*rows, near, far)


def swap(block, axis, distance):
    return lax.ppermute(block, axis, [(i, i ^ distance) for i in range(lax.axis_size(axis))])


def send_to_chip(block, relative):
    sizes = (lax.axis_size("z"), lax.axis_size("x"))
    return lax.ppermute(
        block, ("z", "x"), [(i, i ^ relative) for i in range(sizes[0] * sizes[1])]
    )


def after(value, earlier):
    return lax.optimization_barrier((value, earlier))[0]


def dense_body(hidden, expert_ids, gate_weights, down_weight):
    own = (lax.axis_index("z") * 2 + lax.axis_index("x")) * 2 + lax.axis_index("core")
    near = down_weight[0]
    far = swap(near, "core", 1)
    odd, even = (7, 5, 3, 1), (6, 4, 2, 0)
    arrived = [None] * CHIPS
    blocks = spread_rows(hidden, expert_ids, gate_weights, own, odd)
    for relative, block in zip(odd, blocks):
        arrived[relative] = send_to_chip(block, relative)
    blocks = spread_rows(hidden, expert_ids, gate_weights, own, even, near)
    for relative, block in zip(even, blocks):
        arrived[relative] = send_to_chip(block, relative) if relative else block
    across, last = [], blocks[-1]
    for columns in COLUMNS:
        arrived[1] = after(arrived[1], last)
        last = mix(arrived[1::2], near, far, *columns)
        across.append(swap(last, "x", 1))
    kept, lines, pairs, results = [], [], [], []

    def mix_even(parts):
        start, width = COLUMNS[parts[0]][0], sum(COLUMNS[i][1] for i in parts)
        arrived[0] = after(arrived[0], last)
        block = mix(arrived[0::2], near, far, start, width)
        for i in parts:
            low = COLUMNS[i][0] - start
            kept.append(block[:, :, low : low + COLUMNS[i][1]])
        return block

    def add_x(i, last):
        line = after(kept[i], last).astype(jnp.float32) + across[i].astype(jnp.float32)
        lines.append((line[0::2], swap(line[1::2].astype(jnp.bfloat16), "z", 1)))
        return line

    def add_z(i, last):
        pair = after(lines[i][0], last) + lines[i][1].astype(jnp.float32)
        pairs.append((pair[0], swap(pair[1].astype(jnp.bfloat16), "z", 2)))
        return pair

    last = mix_even((0, 1))
    last = add_x(0, last)
    last = mix_even((2, 3))
    for i in range(1, len(COLUMNS)):
        last = add_x(i, last)
        last = add_z(i - 1, last)
    add_z(len(COLUMNS) - 1, last)
    for mine, theirs in pairs:
        results.append((mine + theirs.astype(jnp.float32)).astype(jnp.bfloat16))
    return jnp.concatenate(results, axis=1)


def solution(mesh):
    groups, owners, tensors = (mesh.shape[axis] for axis in ("groups", "expert", "tensor"))

    def whole(hidden, expert_ids, gate_weights, down_weight):
        tokens = hidden.shape[0] // (groups * owners)
        capacity = 2 * tokens * hidden.shape[1] // down_weight.shape[0]
        one_each = owners == 2 * CHIPS and down_weight.shape[0] == owners
        if tensors == 1 and one_each and capacity >= tokens:
            axes = ("groups", "z", "x", "core")
            used = Mesh(mesh.devices.reshape(groups, CHIPS // 2, 2, 2), axes)
            run, batch = dense_body, P(axes)
            weight, out = P(axes[1:]), P(axes)
        else:
            used, run, batch = mesh, slotted_body, P(("groups", "expert"))
            weight = P("expert", "tensor", None)
            out = P(("groups", "expert"), "tensor")
        rows = batch if tensors == 1 else P(("groups", "expert"), None, "tensor")
        return jax.shard_map(
            run,
            mesh=used,
            in_specs=(rows, batch, batch, weight),
            out_specs=out,
            check_vma=False,
        )(hidden, expert_ids, gate_weights, down_weight)

    return whole
```

```python
import functools

import jax
import jax.numpy as jnp
from jax import lax
from jax.experimental import pallas as pl
from jax.experimental.pallas import tpu as pltpu
from jax.sharding import Mesh, PartitionSpec as P

CHIPS = 8
TILE = 512
COLUMNS = ((0, 1024), (1024, 1536), (2560, 512), (3072, 512))


def passed_along(block, axis, distance):
    devices = range(lax.axis_size(axis))
    route = [((i - distance) % len(devices), i) for i in devices]
    return lax.ppermute(block, axis, route)


def project(arrived, weights):
    return jnp.einsum("secf,efd->secd", arrived, weights, preferred_element_type=jnp.float32)


def slotted_body(hidden, expert_ids, gate_weights, down_weight):
    token_count, choose_count, half_hidden = hidden.shape
    local_experts = down_weight.shape[0]
    owner_count = lax.axis_size("expert")
    tensor_count = lax.axis_size("tensor")
    all_experts = owner_count * local_experts
    capacity = min(token_count, max(2, 2 * token_count * choose_count // all_experts))
    flat_ids = expert_ids.reshape(-1)
    onehot = (flat_ids[:, None] == jnp.arange(all_experts, dtype=jnp.int32)[None, :]).astype(
        jnp.int32
    )
    running = jnp.cumsum(onehot, axis=0)
    ranks = jnp.sum(onehot * running, axis=1) - 1
    slots = flat_ids * capacity + ranks
    copy_rows = hidden.reshape(token_count * choose_count, half_hidden)
    outgoing = (
        jnp.zeros((all_experts * capacity, half_hidden), hidden.dtype).at[slots].set(copy_rows)
    )
    outgoing = outgoing.reshape(owner_count, local_experts, capacity, half_hidden)
    width_total = down_weight.shape[2]
    width_half = width_total // tensor_count
    position = lax.axis_index("tensor")
    other = 1 - position
    arrived = lax.all_to_all(outgoing, "expert", split_axis=0, concat_axis=0, tiled=True)
    if tensor_count == 1:
        summed = project(arrived, down_weight).astype(jnp.bfloat16)
    else:
        partial_rows = project(arrived, down_weight).astype(jnp.bfloat16)
        outbound = lax.dynamic_slice_in_dim(partial_rows, other * width_half, width_half, 3)
        mine = lax.dynamic_slice_in_dim(partial_rows, position * width_half, width_half, 3)
        inbound = passed_along(outbound, "tensor", 1)
        summed = (mine.astype(jnp.float32) + inbound.astype(jnp.float32)).astype(jnp.bfloat16)
    returned = lax.all_to_all(summed, "expert", split_axis=0, concat_axis=0, tiled=True)
    flat_back = returned.reshape(all_experts * capacity, returned.shape[3])
    picked = (
        flat_back[slots].astype(jnp.float32).reshape(token_count, choose_count, returned.shape[3])
    )
    combined = jnp.sum(picked * gate_weights[:, :, None], axis=1)
    return combined.astype(jnp.bfloat16)


def spread_kernel(relatives, own_ref, ids_ref, gates_ref, hidden_ref, *refs):
    out_refs = refs[-len(relatives) :]
    own = own_ref[0]
    choose_count, token_count = ids_ref.shape
    shape = (token_count, token_count * choose_count)
    row = lax.broadcasted_iota(jnp.int32, shape, 0) * choose_count
    column = lax.broadcasted_iota(jnp.int32, shape, 1)
    same = (column >= row) & (column < row + choose_count)
    across = (choose_count, token_count * choose_count)
    choice = lax.rem(lax.broadcasted_iota(jnp.int32, across, 1), choose_count)
    repeat = (choice == lax.broadcasted_iota(jnp.int32, across, 0)).astype(jnp.float32)
    ids, gate_weights = ids_ref[...].T, gates_ref[...].T
    spread_ids = jnp.dot(ids.astype(jnp.float32), repeat, preferred_element_type=jnp.float32)
    own_row = jnp.where(same, (spread_ids + 0.5).astype(jnp.int32), -1)
    for at in range(0, len(relatives), 2):
        picks, gates = [], []
        for relative in relatives[at : at + 2]:
            for core in range(2):
                expert = own ^ (2 * relative + core)
                picks.append((own_row == expert).astype(jnp.float32).astype(hidden_ref.dtype))
                gates.append(
                    jnp.sum(jnp.where(ids == expert, gate_weights, 0.0), axis=1, keepdims=True)
                )
        rows = jnp.dot(
            jnp.concatenate(picks, axis=0), hidden_ref[...], preferred_element_type=jnp.float32
        )
        scaled = (rows * jnp.concatenate(gates, axis=0)).astype(hidden_ref.dtype)
        for place in range(len(picks) // 2):
            block = scaled[2 * place * token_count : 2 * (place + 1) * token_count]
            out_refs[at + place][...] = block.reshape(2, token_count, -1)


def spread_rows(hidden, expert_ids, gate_weights, own, relatives, held=None):
    token_count, choose_count, width = hidden.shape
    vmem = pl.BlockSpec(memory_space=pltpu.VMEM)
    block = jax.ShapeDtypeStruct((2, token_count, width), hidden.dtype)
    more = [] if held is None else [held]
    return pl.pallas_call(
        functools.partial(spread_kernel, relatives),
        in_specs=[pl.BlockSpec(memory_space=pltpu.SMEM)] + [vmem] * (3 + len(more)),
        out_specs=[vmem] * len(relatives),
        out_shape=[block] * len(relatives),
        compiler_params=pltpu.CompilerParams(vmem_limit_bytes=24 << 20),
        cost_estimate=pl.CostEstimate(flops=0, bytes_accessed=0, transcendentals=0),
        name="spread_rows",
    )(
        own.reshape(1),
        expert_ids.T,
        gate_weights.T,
        hidden.reshape(token_count * choose_count, width),
        *more,
    )


def mix_kernel(*refs):
    rows, (near_ref, far_ref, out_ref, joined_ref) = refs[:-4], refs[-4:]
    tokens = rows[0].shape[1]

    @pl.when(pl.program_id(0) == 0)
    def _():
        for place, ref in enumerate(rows):
            joined_ref[:, place * tokens : (place + 1) * tokens] = ref[...]

    total = jnp.dot(joined_ref[0], near_ref[...], preferred_element_type=jnp.float32)
    total += jnp.dot(joined_ref[1], far_ref[...], preferred_element_type=jnp.float32)
    out_ref[...] = total.reshape(len(rows), tokens, -1).astype(out_ref.dtype)


def mix(rows, near, far, start, width):
    _, tokens, depth = rows[0].shape
    whole = pl.BlockSpec((2, tokens, depth), lambda i: (0, 0, 0))
    weight = pl.BlockSpec((depth, TILE), lambda i: (0, start // TILE + i))
    return pl.pallas_call(
        mix_kernel,
        grid=(width // TILE,),
        in_specs=[whole] * len(rows) + [weight] * 2,
        out_specs=pl.BlockSpec((len(rows), tokens, TILE), lambda i: (0, 0, i)),
        out_shape=jax.ShapeDtypeStruct((len(rows), tokens, width), jnp.bfloat16),
        scratch_shapes=[pltpu.VMEM((2, len(rows) * tokens, depth), jnp.bfloat16)],
        compiler_params=pltpu.CompilerParams(vmem_limit_bytes=24 << 20),
        cost_estimate=pl.CostEstimate(flops=4 * len(rows) * tokens * depth * width, bytes_accessed=4 * depth * width, transcendentals=0),
        name="mix",
    )(*rows, near, far)


def swap(block, axis, distance):
    return lax.ppermute(block, axis, [(i, i ^ distance) for i in range(lax.axis_size(axis))])


def send_to_chip(block, relative):
    sizes = (lax.axis_size("z"), lax.axis_size("x"))
    return lax.ppermute(
        block, ("z", "x"), [(i, i ^ relative) for i in range(sizes[0] * sizes[1])]
    )


def after(value, earlier):
    return lax.optimization_barrier((value, earlier))[0]


def dense_body(hidden, expert_ids, gate_weights, down_weight):
    own = (lax.axis_index("z") * 2 + lax.axis_index("x")) * 2 + lax.axis_index("core")
    near = down_weight[0]
    far = swap(near, "core", 1)
    odd, even = (7, 5, 3, 1), (6, 4, 2, 0)
    arrived = [None] * CHIPS
    blocks = spread_rows(hidden, expert_ids, gate_weights, own, odd)
    for relative, block in zip(odd, blocks):
        arrived[relative] = send_to_chip(block, relative)
    blocks = spread_rows(hidden, expert_ids, gate_weights, own, even, near)
    for relative, block in zip(even, blocks):
        arrived[relative] = send_to_chip(block, relative) if relative else block
    across, last = [], blocks[-1]
    for columns in COLUMNS:
        arrived[1] = after(arrived[1], last)
        last = mix(arrived[1::2], near, far, *columns)
        across.append(swap(last, "x", 1))
    kept, lines, pairs, results = [], [], [], []

    def mix_even(parts):
        start, width = COLUMNS[parts[0]][0], sum(COLUMNS[i][1] for i in parts)
        arrived[0] = after(arrived[0], last)
        block = mix(arrived[0::2], near, far, start, width)
        for i in parts:
            low = COLUMNS[i][0] - start
            kept.append(block[:, :, low : low + COLUMNS[i][1]])
        return block

    def add_x(i, last):
        line = after(kept[i], last).astype(jnp.float32) + across[i].astype(jnp.float32)
        lines.append((line[0::2], swap(line[1::2].astype(jnp.bfloat16), "z", 1)))
        return line

    def add_z(i, last):
        pair = after(lines[i][0], last) + lines[i][1].astype(jnp.float32)
        pairs.append((pair[0], swap(pair[1].astype(jnp.bfloat16), "z", 2)))
        return pair

    last = mix_even((0,))
    last = add_x(0, last)
    last = mix_even((1,))
    last = add_x(1, last)
    last = mix_even((2, 3))
    last = add_z(0, last)
    for i in range(2, len(COLUMNS)):
        last = add_x(i, last)
        last = add_z(i - 1, last)
    add_z(len(COLUMNS) - 1, last)
    for mine, theirs in pairs:
        results.append((mine + theirs.astype(jnp.float32)).astype(jnp.bfloat16))
    return jnp.concatenate(results, axis=1)


def solution(mesh):
    groups, owners, tensors = (mesh.shape[axis] for axis in ("groups", "expert", "tensor"))

    def whole(hidden, expert_ids, gate_weights, down_weight):
        tokens = hidden.shape[0] // (groups * owners)
        capacity = 2 * tokens * hidden.shape[1] // down_weight.shape[0]
        one_each = owners == 2 * CHIPS and down_weight.shape[0] == owners
        if tensors == 1 and one_each and capacity >= tokens:
            axes = ("groups", "z", "x", "core")
            used = Mesh(mesh.devices.reshape(groups, CHIPS // 2, 2, 2), axes)
            run, batch = dense_body, P(axes)
            weight, out = P(axes[1:]), P(axes)
        else:
            used, run, batch = mesh, slotted_body, P(("groups", "expert"))
            weight = P("expert", "tensor", None)
            out = P(("groups", "expert"), "tensor")
        rows = batch if tensors == 1 else P(("groups", "expert"), None, "tensor")
        return jax.shard_map(
            run,
            mesh=used,
            in_specs=(rows, batch, batch, weight),
            out_specs=out,
            check_vma=False,
        )(hidden, expert_ids, gate_weights, down_weight)

    return whole
```

```python
import functools

import jax
import jax.numpy as jnp
from jax import lax
from jax.experimental import pallas as pl
from jax.experimental.pallas import tpu as pltpu
from jax.sharding import Mesh, PartitionSpec as P

CHIPS = 8
TILE = 512
COLUMNS = ((0, 1024), (1024, 1536), (2560, 512), (3072, 512))
LIGHT, HEAVY = 0.01, 4.0


def passed_along(block, axis, distance):
    devices = range(lax.axis_size(axis))
    route = [((i - distance) % len(devices), i) for i in devices]
    return lax.ppermute(block, axis, route)


def project(arrived, weights):
    return jnp.einsum("secf,efd->secd", arrived, weights, preferred_element_type=jnp.float32)


def slotted_body(hidden, expert_ids, gate_weights, down_weight):
    token_count, choose_count, half_hidden = hidden.shape
    local_experts = down_weight.shape[0]
    owner_count = lax.axis_size("expert")
    tensor_count = lax.axis_size("tensor")
    all_experts = owner_count * local_experts
    capacity = min(token_count, max(2, 2 * token_count * choose_count // all_experts))
    flat_ids = expert_ids.reshape(-1)
    onehot = (flat_ids[:, None] == jnp.arange(all_experts, dtype=jnp.int32)[None, :]).astype(
        jnp.int32
    )
    running = jnp.cumsum(onehot, axis=0)
    ranks = jnp.sum(onehot * running, axis=1) - 1
    slots = flat_ids * capacity + ranks
    copy_rows = hidden.reshape(token_count * choose_count, half_hidden)
    outgoing = (
        jnp.zeros((all_experts * capacity, half_hidden), hidden.dtype).at[slots].set(copy_rows)
    )
    outgoing = outgoing.reshape(owner_count, local_experts, capacity, half_hidden)
    width_total = down_weight.shape[2]
    width_half = width_total // tensor_count
    position = lax.axis_index("tensor")
    other = 1 - position
    arrived = lax.all_to_all(outgoing, "expert", split_axis=0, concat_axis=0, tiled=True)
    if tensor_count == 1:
        summed = project(arrived, down_weight).astype(jnp.bfloat16)
    else:
        partial_rows = project(arrived, down_weight).astype(jnp.bfloat16)
        outbound = lax.dynamic_slice_in_dim(partial_rows, other * width_half, width_half, 3)
        mine = lax.dynamic_slice_in_dim(partial_rows, position * width_half, width_half, 3)
        inbound = passed_along(outbound, "tensor", 1)
        summed = (mine.astype(jnp.float32) + inbound.astype(jnp.float32)).astype(jnp.bfloat16)
    returned = lax.all_to_all(summed, "expert", split_axis=0, concat_axis=0, tiled=True)
    flat_back = returned.reshape(all_experts * capacity, returned.shape[3])
    picked = (
        flat_back[slots].astype(jnp.float32).reshape(token_count, choose_count, returned.shape[3])
    )
    combined = jnp.sum(picked * gate_weights[:, :, None], axis=1)
    return combined.astype(jnp.bfloat16)


def spread_kernel(relatives, own_ref, ids_ref, gates_ref, hidden_ref, *refs):
    out_refs = refs[-len(relatives) :]
    own = own_ref[0]
    choose_count, token_count = ids_ref.shape
    shape = (token_count, token_count * choose_count)
    row = lax.broadcasted_iota(jnp.int32, shape, 0) * choose_count
    column = lax.broadcasted_iota(jnp.int32, shape, 1)
    same = (column >= row) & (column < row + choose_count)
    across = (choose_count, token_count * choose_count)
    choice = lax.rem(lax.broadcasted_iota(jnp.int32, across, 1), choose_count)
    repeat = (choice == lax.broadcasted_iota(jnp.int32, across, 0)).astype(jnp.float32)
    ids, gate_weights = ids_ref[...].T, gates_ref[...].T
    spread_ids = jnp.dot(ids.astype(jnp.float32), repeat, preferred_element_type=jnp.float32)
    own_row = jnp.where(same, (spread_ids + 0.5).astype(jnp.int32), -1)
    for at in range(0, len(relatives), 2):
        picks, gates = [], []
        for relative in relatives[at : at + 2]:
            for core in range(2):
                expert = own ^ (2 * relative + core)
                picks.append((own_row == expert).astype(jnp.float32).astype(hidden_ref.dtype))
                gates.append(
                    jnp.sum(jnp.where(ids == expert, gate_weights, 0.0), axis=1, keepdims=True)
                )
        rows = jnp.dot(
            jnp.concatenate(picks, axis=0), hidden_ref[...], preferred_element_type=jnp.float32
        )
        scaled = (rows * jnp.concatenate(gates, axis=0)).astype(hidden_ref.dtype)
        for place in range(len(picks) // 2):
            block = scaled[2 * place * token_count : 2 * (place + 1) * token_count]
            out_refs[at + place][...] = block.reshape(2, token_count, -1)


def spread_rows(hidden, expert_ids, gate_weights, own, relatives, held=None):
    token_count, choose_count, width = hidden.shape
    vmem = pl.BlockSpec(memory_space=pltpu.VMEM)
    block = jax.ShapeDtypeStruct((2, token_count, width), hidden.dtype)
    more = [] if held is None else [held]
    return pl.pallas_call(
        functools.partial(spread_kernel, relatives),
        in_specs=[pl.BlockSpec(memory_space=pltpu.SMEM)] + [vmem] * (3 + len(more)),
        out_specs=[vmem] * len(relatives),
        out_shape=[block] * len(relatives),
        compiler_params=pltpu.CompilerParams(vmem_limit_bytes=24 << 20),
        cost_estimate=pl.CostEstimate(flops=0, bytes_accessed=0, transcendentals=0),
        name="spread_rows",
    )(
        own.reshape(1),
        expert_ids.T,
        gate_weights.T,
        hidden.reshape(token_count * choose_count, width),
        *more,
    )


def mix_kernel(*refs):
    rows, (near_ref, far_ref, out_ref, joined_ref) = refs[:-4], refs[-4:]
    tokens = rows[0].shape[1]

    @pl.when(pl.program_id(0) == 0)
    def _():
        for place, ref in enumerate(rows):
            joined_ref[:, place * tokens : (place + 1) * tokens] = ref[...]

    total = jnp.dot(joined_ref[0], near_ref[...], preferred_element_type=jnp.float32)
    total += jnp.dot(joined_ref[1], far_ref[...], preferred_element_type=jnp.float32)
    out_ref[...] = total.reshape(len(rows), tokens, -1).astype(out_ref.dtype)


def mix(rows, near, far, start, width, weight_of_cost):
    _, tokens, depth = rows[0].shape
    whole = pl.BlockSpec((2, tokens, depth), lambda i: (0, 0, 0))
    weight = pl.BlockSpec((depth, TILE), lambda i: (0, start // TILE + i))
    return pl.pallas_call(
        mix_kernel,
        grid=(width // TILE,),
        in_specs=[whole] * len(rows) + [weight] * 2,
        out_specs=pl.BlockSpec((len(rows), tokens, TILE), lambda i: (0, 0, i)),
        out_shape=jax.ShapeDtypeStruct((len(rows), tokens, width), jnp.bfloat16),
        scratch_shapes=[pltpu.VMEM((2, len(rows) * tokens, depth), jnp.bfloat16)],
        compiler_params=pltpu.CompilerParams(vmem_limit_bytes=24 << 20),
        cost_estimate=pl.CostEstimate(
            flops=int(weight_of_cost * 4 * len(rows) * tokens * depth * width),
            bytes_accessed=int(weight_of_cost * 4 * depth * width),
            transcendentals=0,
        ),
        name="mix",
    )(*rows, near, far)


def swap(block, axis, distance):
    return lax.ppermute(block, axis, [(i, i ^ distance) for i in range(lax.axis_size(axis))])


def send_to_chip(block, relative):
    sizes = (lax.axis_size("z"), lax.axis_size("x"))
    return lax.ppermute(
        block, ("z", "x"), [(i, i ^ relative) for i in range(sizes[0] * sizes[1])]
    )


def after(value, earlier):
    return lax.optimization_barrier((value, earlier))[0]


def dense_body(hidden, expert_ids, gate_weights, down_weight):
    own = (lax.axis_index("z") * 2 + lax.axis_index("x")) * 2 + lax.axis_index("core")
    near = down_weight[0]
    far = swap(near, "core", 1)
    odd, even = (7, 5, 3, 1), (6, 4, 2, 0)
    arrived = [None] * CHIPS
    blocks = spread_rows(hidden, expert_ids, gate_weights, own, odd)
    for relative, block in zip(odd, blocks):
        arrived[relative] = send_to_chip(block, relative)
    blocks = spread_rows(hidden, expert_ids, gate_weights, own, even, near)
    for relative, block in zip(even, blocks):
        arrived[relative] = send_to_chip(block, relative) if relative else block
    across, kept, lines, pairs, results = [], [], [], [], []

    def mix_odd(i, earlier):
        arrived[7] = after(arrived[7], earlier)
        block = mix([arrived[r] for r in odd], near, far, *COLUMNS[i], LIGHT)
        across.append(swap(block, "x", 1))
        return block

    def mix_even(parts, earlier, weight):
        start, width = COLUMNS[parts[0]][0], sum(COLUMNS[i][1] for i in parts)
        arrived[0] = after(arrived[0], earlier)
        block = mix([arrived[r] for r in even], near, far, start, width, weight)
        for i in parts:
            low = COLUMNS[i][0] - start
            kept.append(block[:, :, low : low + COLUMNS[i][1]])
        return block

    def add_x(i, earlier):
        line = after(kept[i], earlier).astype(jnp.float32) + across[i].astype(jnp.float32)
        lines.append((line[1::2], swap(line[0::2].astype(jnp.bfloat16), "z", 1)))
        return line

    def add_z(i, earlier):
        pair = after(lines[i][0], earlier) + lines[i][1].astype(jnp.float32)
        pairs.append((pair[1], swap(pair[0].astype(jnp.bfloat16), "z", 2)))
        return pair

    last = mix_odd(0, blocks[-1])
    last = mix_odd(1, last)
    last = mix_even((0,), last, HEAVY)
    last = add_x(0, last)
    last = mix_odd(2, last)
    last = mix_even((1,), last, LIGHT)
    last = add_x(1, last)
    last = mix_odd(3, last)
    last = mix_even((2, 3), last, LIGHT)
    last = add_z(0, last)
    for i in range(2, len(COLUMNS)):
        last = add_x(i, last)
        last = add_z(i - 1, last)
    add_z(len(COLUMNS) - 1, last)
    for mine, theirs in pairs:
        results.append((mine + theirs.astype(jnp.float32)).astype(jnp.bfloat16))
    return jnp.concatenate(results, axis=1)


def solution(mesh):
    groups, owners, tensors = (mesh.shape[axis] for axis in ("groups", "expert", "tensor"))

    def whole(hidden, expert_ids, gate_weights, down_weight):
        tokens = hidden.shape[0] // (groups * owners)
        capacity = 2 * tokens * hidden.shape[1] // down_weight.shape[0]
        one_each = owners == 2 * CHIPS and down_weight.shape[0] == owners
        if tensors == 1 and one_each and capacity >= tokens:
            axes = ("groups", "z", "x", "core")
            used = Mesh(mesh.devices.reshape(groups, CHIPS // 2, 2, 2), axes)
            run, batch = dense_body, P(axes)
            weight, out = P(axes[1:]), P(axes)
        else:
            used, run, batch = mesh, slotted_body, P(("groups", "expert"))
            weight = P("expert", "tensor", None)
            out = P(("groups", "expert"), "tensor")
        rows = batch if tensors == 1 else P(("groups", "expert"), None, "tensor")
        return jax.shard_map(
            run,
            mesh=used,
            in_specs=(rows, batch, batch, weight),
            out_specs=out,
            check_vma=False,
        )(hidden, expert_ids, gate_weights, down_weight)

    return whole
```

```python
import functools

import jax
import jax.numpy as jnp
from jax import lax
from jax.experimental import pallas as pl
from jax.experimental.pallas import tpu as pltpu
from jax.sharding import Mesh, PartitionSpec as P

CHIPS = 8
TILE = 512
COLUMNS = ((0, 1024), (1024, 1536), (2560, 1024))
LIGHT, HEAVY = 0.01, 4.0


def passed_along(block, axis, distance):
    devices = range(lax.axis_size(axis))
    route = [((i - distance) % len(devices), i) for i in devices]
    return lax.ppermute(block, axis, route)


def project(arrived, weights):
    return jnp.einsum("secf,efd->secd", arrived, weights, preferred_element_type=jnp.float32)


def slotted_body(hidden, expert_ids, gate_weights, down_weight):
    token_count, choose_count, half_hidden = hidden.shape
    local_experts = down_weight.shape[0]
    owner_count = lax.axis_size("expert")
    tensor_count = lax.axis_size("tensor")
    all_experts = owner_count * local_experts
    capacity = min(token_count, max(2, 2 * token_count * choose_count // all_experts))
    flat_ids = expert_ids.reshape(-1)
    onehot = (flat_ids[:, None] == jnp.arange(all_experts, dtype=jnp.int32)[None, :]).astype(
        jnp.int32
    )
    running = jnp.cumsum(onehot, axis=0)
    ranks = jnp.sum(onehot * running, axis=1) - 1
    slots = flat_ids * capacity + ranks
    copy_rows = hidden.reshape(token_count * choose_count, half_hidden)
    outgoing = (
        jnp.zeros((all_experts * capacity, half_hidden), hidden.dtype).at[slots].set(copy_rows)
    )
    outgoing = outgoing.reshape(owner_count, local_experts, capacity, half_hidden)
    width_total = down_weight.shape[2]
    width_half = width_total // tensor_count
    position = lax.axis_index("tensor")
    other = 1 - position
    arrived = lax.all_to_all(outgoing, "expert", split_axis=0, concat_axis=0, tiled=True)
    if tensor_count == 1:
        summed = project(arrived, down_weight).astype(jnp.bfloat16)
    else:
        partial_rows = project(arrived, down_weight).astype(jnp.bfloat16)
        outbound = lax.dynamic_slice_in_dim(partial_rows, other * width_half, width_half, 3)
        mine = lax.dynamic_slice_in_dim(partial_rows, position * width_half, width_half, 3)
        inbound = passed_along(outbound, "tensor", 1)
        summed = (mine.astype(jnp.float32) + inbound.astype(jnp.float32)).astype(jnp.bfloat16)
    returned = lax.all_to_all(summed, "expert", split_axis=0, concat_axis=0, tiled=True)
    flat_back = returned.reshape(all_experts * capacity, returned.shape[3])
    picked = (
        flat_back[slots].astype(jnp.float32).reshape(token_count, choose_count, returned.shape[3])
    )
    combined = jnp.sum(picked * gate_weights[:, :, None], axis=1)
    return combined.astype(jnp.bfloat16)


def spread_kernel(relatives, own_ref, ids_ref, gates_ref, hidden_ref, *refs):
    out_refs = refs[-len(relatives) :]
    own = own_ref[0]
    choose_count, token_count = ids_ref.shape
    shape = (token_count, token_count * choose_count)
    row = lax.broadcasted_iota(jnp.int32, shape, 0) * choose_count
    column = lax.broadcasted_iota(jnp.int32, shape, 1)
    same = (column >= row) & (column < row + choose_count)
    across = (choose_count, token_count * choose_count)
    choice = lax.rem(lax.broadcasted_iota(jnp.int32, across, 1), choose_count)
    repeat = (choice == lax.broadcasted_iota(jnp.int32, across, 0)).astype(jnp.float32)
    ids, gate_weights = ids_ref[...].T, gates_ref[...].T
    spread_ids = jnp.dot(ids.astype(jnp.float32), repeat, preferred_element_type=jnp.float32)
    own_row = jnp.where(same, (spread_ids + 0.5).astype(jnp.int32), -1)
    for at in range(0, len(relatives), 2):
        picks, gates = [], []
        for relative in relatives[at : at + 2]:
            for core in range(2):
                expert = own ^ (2 * relative + core)
                picks.append((own_row == expert).astype(jnp.float32).astype(hidden_ref.dtype))
                gates.append(
                    jnp.sum(jnp.where(ids == expert, gate_weights, 0.0), axis=1, keepdims=True)
                )
        rows = jnp.dot(
            jnp.concatenate(picks, axis=0), hidden_ref[...], preferred_element_type=jnp.float32
        )
        scaled = (rows * jnp.concatenate(gates, axis=0)).astype(hidden_ref.dtype)
        for place in range(len(picks) // 2):
            block = scaled[2 * place * token_count : 2 * (place + 1) * token_count]
            out_refs[at + place][...] = block.reshape(2, token_count, -1)


def spread_rows(hidden, expert_ids, gate_weights, own, relatives, held=None):
    token_count, choose_count, width = hidden.shape
    vmem = pl.BlockSpec(memory_space=pltpu.VMEM)
    block = jax.ShapeDtypeStruct((2, token_count, width), hidden.dtype)
    more = [] if held is None else [held]
    return pl.pallas_call(
        functools.partial(spread_kernel, relatives),
        in_specs=[pl.BlockSpec(memory_space=pltpu.SMEM)] + [vmem] * (3 + len(more)),
        out_specs=[vmem] * len(relatives),
        out_shape=[block] * len(relatives),
        compiler_params=pltpu.CompilerParams(vmem_limit_bytes=24 << 20),
        cost_estimate=pl.CostEstimate(flops=0, bytes_accessed=0, transcendentals=0),
        name="spread_rows",
    )(
        own.reshape(1),
        expert_ids.T,
        gate_weights.T,
        hidden.reshape(token_count * choose_count, width),
        *more,
    )


def mix_kernel(*refs):
    rows, (near_ref, far_ref, out_ref, joined_ref) = refs[:-4], refs[-4:]
    tokens = rows[0].shape[1]

    @pl.when(pl.program_id(0) == 0)
    def _():
        for place, ref in enumerate(rows):
            joined_ref[:, place * tokens : (place + 1) * tokens] = ref[...]

    total = jnp.dot(joined_ref[0], near_ref[...], preferred_element_type=jnp.float32)
    total += jnp.dot(joined_ref[1], far_ref[...], preferred_element_type=jnp.float32)
    out_ref[...] = total.reshape(len(rows), tokens, -1).astype(out_ref.dtype)


def mix(rows, near, far, start, width, weight_of_cost):
    _, tokens, depth = rows[0].shape
    whole = pl.BlockSpec((2, tokens, depth), lambda i: (0, 0, 0))
    weight = pl.BlockSpec((depth, TILE), lambda i: (0, start // TILE + i))
    return pl.pallas_call(
        mix_kernel,
        grid=(width // TILE,),
        in_specs=[whole] * len(rows) + [weight] * 2,
        out_specs=pl.BlockSpec((len(rows), tokens, TILE), lambda i: (0, 0, i)),
        out_shape=jax.ShapeDtypeStruct((len(rows), tokens, width), jnp.bfloat16),
        scratch_shapes=[pltpu.VMEM((2, len(rows) * tokens, depth), jnp.bfloat16)],
        compiler_params=pltpu.CompilerParams(vmem_limit_bytes=24 << 20),
        cost_estimate=pl.CostEstimate(
            flops=int(weight_of_cost * 4 * len(rows) * tokens * depth * width),
            bytes_accessed=int(weight_of_cost * 4 * depth * width),
            transcendentals=0,
        ),
        name="mix",
    )(*rows, near, far)


def swap(block, axis, distance):
    return lax.ppermute(block, axis, [(i, i ^ distance) for i in range(lax.axis_size(axis))])


def send_to_chip(block, relative):
    sizes = (lax.axis_size("z"), lax.axis_size("x"))
    return lax.ppermute(
        block, ("z", "x"), [(i, i ^ relative) for i in range(sizes[0] * sizes[1])]
    )


def after(value, earlier):
    return lax.optimization_barrier((value, earlier))[0]


def dense_body(hidden, expert_ids, gate_weights, down_weight):
    own = (lax.axis_index("z") * 2 + lax.axis_index("x")) * 2 + lax.axis_index("core")
    near = down_weight[0]
    far = swap(near, "core", 1)
    odd, even = (7, 5, 3, 1), (6, 4, 2, 0)
    arrived = [None] * CHIPS
    blocks = spread_rows(hidden, expert_ids, gate_weights, own, odd)
    for relative, block in zip(odd, blocks):
        arrived[relative] = send_to_chip(block, relative)
    blocks = spread_rows(hidden, expert_ids, gate_weights, own, even, near)
    blocks = after(blocks, [arrived[r] for r in odd])
    for relative, block in zip(even, blocks):
        arrived[relative] = send_to_chip(block, relative) if relative else block
    across, kept, lines, pairs, results = [], [], [], [], []

    def mix_odd(i, earlier):
        arrived[7] = after(arrived[7], earlier)
        block = mix([arrived[r] for r in odd], near, far, *COLUMNS[i], LIGHT)
        across.append(swap(block, "x", 1))
        return block

    def mix_even(parts, earlier, weight):
        start, width = COLUMNS[parts[0]][0], sum(COLUMNS[i][1] for i in parts)
        arrived[0] = after(arrived[0], earlier)
        block = mix([arrived[r] for r in even], near, far, start, width, weight)
        for i in parts:
            low = COLUMNS[i][0] - start
            kept.append(block[:, :, low : low + COLUMNS[i][1]])
        return block

    def add_x(i, earlier):
        line = after(kept[i], earlier).astype(jnp.float32) + across[i].astype(jnp.float32)
        lines.append((line[1::2], swap(line[0::2].astype(jnp.bfloat16), "z", 1)))
        return line

    def add_z(i, earlier):
        pair = after(lines[i][0], earlier) + lines[i][1].astype(jnp.float32)
        pairs.append((pair[1], swap(pair[0].astype(jnp.bfloat16), "z", 2)))
        return pair

    last = mix_odd(0, blocks[-1])
    last = mix_odd(1, last)
    last = mix_even((0,), last, HEAVY)
    last = add_x(0, last)
    last = mix_odd(2, last)
    last = mix_even((1,), last, LIGHT)
    last = add_x(1, last)
    last = add_z(0, last)
    last = mix_even((2,), last, LIGHT)
    for i in range(2, len(COLUMNS)):
        last = add_x(i, last)
        last = add_z(i - 1, last)
    add_z(len(COLUMNS) - 1, last)
    for mine, theirs in pairs:
        results.append((mine + theirs.astype(jnp.float32)).astype(jnp.bfloat16))
    return jnp.concatenate(results, axis=1)


def solution(mesh):
    groups, owners, tensors = (mesh.shape[axis] for axis in ("groups", "expert", "tensor"))

    def whole(hidden, expert_ids, gate_weights, down_weight):
        tokens = hidden.shape[0] // (groups * owners)
        capacity = 2 * tokens * hidden.shape[1] // down_weight.shape[0]
        one_each = owners == 2 * CHIPS and down_weight.shape[0] == owners
        if tensors == 1 and one_each and capacity >= tokens:
            axes = ("groups", "z", "x", "core")
            used = Mesh(mesh.devices.reshape(groups, CHIPS // 2, 2, 2), axes)
            run, batch = dense_body, P(axes)
            weight, out = P(axes[1:]), P(axes)
        else:
            used, run, batch = mesh, slotted_body, P(("groups", "expert"))
            weight = P("expert", "tensor", None)
            out = P(("groups", "expert"), "tensor")
        rows = batch if tensors == 1 else P(("groups", "expert"), None, "tensor")
        return jax.shard_map(
            run,
            mesh=used,
            in_specs=(rows, batch, batch, weight),
            out_specs=out,
            check_vma=False,
        )(hidden, expert_ids, gate_weights, down_weight)

    return whole
```

```python
import functools

import jax
import jax.numpy as jnp
from jax import lax
from jax.experimental import pallas as pl
from jax.experimental.pallas import tpu as pltpu
from jax.sharding import Mesh, PartitionSpec as P

CHIPS = 8
TILE = 512
COLUMNS = ((0, 1536), (1536, 1536), (3072, 512))
LIGHT = 0.01


def passed_along(block, axis, distance):
    devices = range(lax.axis_size(axis))
    route = [((i - distance) % len(devices), i) for i in devices]
    return lax.ppermute(block, axis, route)


def project(arrived, weights):
    return jnp.einsum("secf,efd->secd", arrived, weights, preferred_element_type=jnp.float32)


def slotted_body(hidden, expert_ids, gate_weights, down_weight):
    token_count, choose_count, half_hidden = hidden.shape
    local_experts = down_weight.shape[0]
    owner_count = lax.axis_size("expert")
    tensor_count = lax.axis_size("tensor")
    all_experts = owner_count * local_experts
    capacity = min(token_count, max(2, 2 * token_count * choose_count // all_experts))
    flat_ids = expert_ids.reshape(-1)
    onehot = (flat_ids[:, None] == jnp.arange(all_experts, dtype=jnp.int32)[None, :]).astype(
        jnp.int32
    )
    running = jnp.cumsum(onehot, axis=0)
    ranks = jnp.sum(onehot * running, axis=1) - 1
    slots = flat_ids * capacity + ranks
    copy_rows = hidden.reshape(token_count * choose_count, half_hidden)
    outgoing = (
        jnp.zeros((all_experts * capacity, half_hidden), hidden.dtype).at[slots].set(copy_rows)
    )
    outgoing = outgoing.reshape(owner_count, local_experts, capacity, half_hidden)
    width_total = down_weight.shape[2]
    width_half = width_total // tensor_count
    position = lax.axis_index("tensor")
    other = 1 - position
    arrived = lax.all_to_all(outgoing, "expert", split_axis=0, concat_axis=0, tiled=True)
    if tensor_count == 1:
        summed = project(arrived, down_weight).astype(jnp.bfloat16)
    else:
        partial_rows = project(arrived, down_weight).astype(jnp.bfloat16)
        outbound = lax.dynamic_slice_in_dim(partial_rows, other * width_half, width_half, 3)
        mine = lax.dynamic_slice_in_dim(partial_rows, position * width_half, width_half, 3)
        inbound = passed_along(outbound, "tensor", 1)
        summed = (mine.astype(jnp.float32) + inbound.astype(jnp.float32)).astype(jnp.bfloat16)
    returned = lax.all_to_all(summed, "expert", split_axis=0, concat_axis=0, tiled=True)
    flat_back = returned.reshape(all_experts * capacity, returned.shape[3])
    picked = (
        flat_back[slots].astype(jnp.float32).reshape(token_count, choose_count, returned.shape[3])
    )
    combined = jnp.sum(picked * gate_weights[:, :, None], axis=1)
    return combined.astype(jnp.bfloat16)


def spread_kernel(relatives, own_ref, ids_ref, gates_ref, hidden_ref, *refs):
    out_refs = refs[-len(relatives) :]
    own = own_ref[0]
    choose_count, token_count = ids_ref.shape
    shape = (token_count, token_count * choose_count)
    row = lax.broadcasted_iota(jnp.int32, shape, 0) * choose_count
    column = lax.broadcasted_iota(jnp.int32, shape, 1)
    same = (column >= row) & (column < row + choose_count)
    across = (choose_count, token_count * choose_count)
    choice = lax.rem(lax.broadcasted_iota(jnp.int32, across, 1), choose_count)
    repeat = (choice == lax.broadcasted_iota(jnp.int32, across, 0)).astype(jnp.float32)
    ids, gate_weights = ids_ref[...].T, gates_ref[...].T
    spread_ids = jnp.dot(ids.astype(jnp.float32), repeat, preferred_element_type=jnp.float32)
    own_row = jnp.where(same, (spread_ids + 0.5).astype(jnp.int32), -1)
    for at in range(0, len(relatives), 2):
        picks, gates = [], []
        for relative in relatives[at : at + 2]:
            for core in range(2):
                expert = own ^ (2 * relative + core)
                picks.append((own_row == expert).astype(jnp.float32).astype(hidden_ref.dtype))
                gates.append(
                    jnp.sum(jnp.where(ids == expert, gate_weights, 0.0), axis=1, keepdims=True)
                )
        rows = jnp.dot(
            jnp.concatenate(picks, axis=0), hidden_ref[...], preferred_element_type=jnp.float32
        )
        scaled = (rows * jnp.concatenate(gates, axis=0)).astype(hidden_ref.dtype)
        for place in range(len(picks) // 2):
            block = scaled[2 * place * token_count : 2 * (place + 1) * token_count]
            out_refs[at + place][...] = block.reshape(2, token_count, -1)


def spread_rows(hidden, expert_ids, gate_weights, own, relatives, held=None):
    token_count, choose_count, width = hidden.shape
    vmem = pl.BlockSpec(memory_space=pltpu.VMEM)
    block = jax.ShapeDtypeStruct((2, token_count, width), hidden.dtype)
    more = [] if held is None else [held]
    return pl.pallas_call(
        functools.partial(spread_kernel, relatives),
        in_specs=[pl.BlockSpec(memory_space=pltpu.SMEM)] + [vmem] * (3 + len(more)),
        out_specs=[vmem] * len(relatives),
        out_shape=[block] * len(relatives),
        compiler_params=pltpu.CompilerParams(vmem_limit_bytes=24 << 20),
        cost_estimate=pl.CostEstimate(flops=0, bytes_accessed=0, transcendentals=0),
        name="spread_rows",
    )(
        own.reshape(1),
        expert_ids.T,
        gate_weights.T,
        hidden.reshape(token_count * choose_count, width),
        *more,
    )


def mix_kernel(*refs):
    rows, (near_ref, far_ref, out_ref, joined_ref) = refs[:-4], refs[-4:]
    tokens = rows[0].shape[1]

    @pl.when(pl.program_id(0) == 0)
    def _():
        for place, ref in enumerate(rows):
            joined_ref[:, place * tokens : (place + 1) * tokens] = ref[...]

    total = jnp.dot(joined_ref[0], near_ref[...], preferred_element_type=jnp.float32)
    total += jnp.dot(joined_ref[1], far_ref[...], preferred_element_type=jnp.float32)
    out_ref[...] = total.reshape(len(rows), tokens, -1).astype(out_ref.dtype)


def mix(rows, near, far, start, width, weight_of_cost):
    _, tokens, depth = rows[0].shape
    whole = pl.BlockSpec((2, tokens, depth), lambda i: (0, 0, 0))
    weight = pl.BlockSpec((depth, TILE), lambda i: (0, start // TILE + i))
    return pl.pallas_call(
        mix_kernel,
        grid=(width // TILE,),
        in_specs=[whole] * len(rows) + [weight] * 2,
        out_specs=pl.BlockSpec((len(rows), tokens, TILE), lambda i: (0, 0, i)),
        out_shape=jax.ShapeDtypeStruct((len(rows), tokens, width), jnp.bfloat16),
        scratch_shapes=[pltpu.VMEM((2, len(rows) * tokens, depth), jnp.bfloat16)],
        compiler_params=pltpu.CompilerParams(vmem_limit_bytes=24 << 20),
        cost_estimate=pl.CostEstimate(
            flops=int(weight_of_cost * 4 * len(rows) * tokens * depth * width),
            bytes_accessed=int(weight_of_cost * 4 * depth * width),
            transcendentals=0,
        ),
        name="mix",
    )(*rows, near, far)


def swap(block, axis, distance):
    return lax.ppermute(block, axis, [(i, i ^ distance) for i in range(lax.axis_size(axis))])


def send_to_chip(block, relative):
    sizes = (lax.axis_size("z"), lax.axis_size("x"))
    return lax.ppermute(
        block, ("z", "x"), [(i, i ^ relative) for i in range(sizes[0] * sizes[1])]
    )


def after(value, earlier):
    return lax.optimization_barrier((value, earlier))[0]


def dense_body(hidden, expert_ids, gate_weights, down_weight):
    own = (lax.axis_index("z") * 2 + lax.axis_index("x")) * 2 + lax.axis_index("core")
    near = down_weight[0]
    far = swap(near, "core", 1)
    odd, even = (7, 5, 3, 1), (6, 4, 2, 0)
    arrived = [None] * CHIPS
    blocks = spread_rows(hidden, expert_ids, gate_weights, own, odd)
    for relative, block in zip(odd, blocks):
        arrived[relative] = send_to_chip(block, relative)
    blocks = spread_rows(hidden, expert_ids, gate_weights, own, even, near)
    blocks = after(blocks, [arrived[r] for r in odd])
    for relative, block in zip(even, blocks):
        arrived[relative] = send_to_chip(block, relative) if relative else block
    given, kept, lines, pairs, results = [], [], [], [], []

    def mix_odd(i, earlier):
        arrived[7] = after(arrived[7], earlier)
        block = mix([arrived[r] for r in odd], near, far, *COLUMNS[i], LIGHT)
        given.append(block)
        return block

    def mix_even(parts, earlier, weight):
        start, width = COLUMNS[parts[0]][0], sum(COLUMNS[i][1] for i in parts)
        arrived[0] = after(arrived[0], earlier)
        block = mix([arrived[r] for r in even], near, far, start, width, weight)
        for i in parts:
            low = COLUMNS[i][0] - start
            kept.append(block[:, :, low : low + COLUMNS[i][1]])
        return block

    def add_x(i, earlier):
        line = after(kept[i], earlier).astype(jnp.float32) + across[i].astype(jnp.float32)
        lines.append((line[1::2], swap(line[0::2].astype(jnp.bfloat16), "z", 1)))
        return line

    def add_z(i, earlier):
        pair = after(lines[i][0], earlier) + lines[i][1].astype(jnp.float32)
        pairs.append((pair[1], swap(pair[0].astype(jnp.bfloat16), "z", 2)))
        return pair

    last = blocks[-1]
    for i in range(len(COLUMNS)):
        last = mix_odd(i, last)
    across = [swap(block, "x", 1) for block in given]
    last = mix_even((0,), last, LIGHT)
    last = add_x(0, last)
    last = mix_even((1,), last, LIGHT)
    last = mix_even((2,), last, LIGHT)
    last = add_x(1, last)
    last = add_z(0, last)
    last = add_x(2, last)
    last = add_z(1, last)
    add_z(2, last)
    for mine, theirs in pairs:
        results.append((mine + theirs.astype(jnp.float32)).astype(jnp.bfloat16))
    return jnp.concatenate(results, axis=1)


def solution(mesh):
    groups, owners, tensors = (mesh.shape[axis] for axis in ("groups", "expert", "tensor"))

    def whole(hidden, expert_ids, gate_weights, down_weight):
        tokens = hidden.shape[0] // (groups * owners)
        capacity = 2 * tokens * hidden.shape[1] // down_weight.shape[0]
        one_each = owners == 2 * CHIPS and down_weight.shape[0] == owners
        if tensors == 1 and one_each and capacity >= tokens:
            axes = ("groups", "z", "x", "core")
            used = Mesh(mesh.devices.reshape(groups, CHIPS // 2, 2, 2), axes)
            run, batch = dense_body, P(axes)
            weight, out = P(axes[1:]), P(axes)
        else:
            used, run, batch = mesh, slotted_body, P(("groups", "expert"))
            weight = P("expert", "tensor", None)
            out = P(("groups", "expert"), "tensor")
        rows = batch if tensors == 1 else P(("groups", "expert"), None, "tensor")
        return jax.shard_map(
            run,
            mesh=used,
            in_specs=(rows, batch, batch, weight),
            out_specs=out,
            check_vma=False,
        )(hidden, expert_ids, gate_weights, down_weight)

    return whole
```

```python
import functools

import jax
import jax.numpy as jnp
from jax import lax
from jax.experimental import pallas as pl
from jax.experimental.pallas import tpu as pltpu
from jax.sharding import Mesh, PartitionSpec as P

CHIPS = 8
TILE = 512
COLUMNS = ((0, 1024), (1024, 1536), (2560, 1024))
LIGHT, HEAVY = 0.01, 3.0


def passed_along(block, axis, distance):
    devices = range(lax.axis_size(axis))
    route = [((i - distance) % len(devices), i) for i in devices]
    return lax.ppermute(block, axis, route)


def project(arrived, weights):
    return jnp.einsum("secf,efd->secd", arrived, weights, preferred_element_type=jnp.float32)


def slotted_body(hidden, expert_ids, gate_weights, down_weight):
    token_count, choose_count, half_hidden = hidden.shape
    local_experts = down_weight.shape[0]
    owner_count = lax.axis_size("expert")
    tensor_count = lax.axis_size("tensor")
    all_experts = owner_count * local_experts
    capacity = min(token_count, max(2, 2 * token_count * choose_count // all_experts))
    flat_ids = expert_ids.reshape(-1)
    onehot = (flat_ids[:, None] == jnp.arange(all_experts, dtype=jnp.int32)[None, :]).astype(
        jnp.int32
    )
    running = jnp.cumsum(onehot, axis=0)
    ranks = jnp.sum(onehot * running, axis=1) - 1
    slots = flat_ids * capacity + ranks
    copy_rows = hidden.reshape(token_count * choose_count, half_hidden)
    outgoing = (
        jnp.zeros((all_experts * capacity, half_hidden), hidden.dtype).at[slots].set(copy_rows)
    )
    outgoing = outgoing.reshape(owner_count, local_experts, capacity, half_hidden)
    width_total = down_weight.shape[2]
    width_half = width_total // tensor_count
    position = lax.axis_index("tensor")
    other = 1 - position
    arrived = lax.all_to_all(outgoing, "expert", split_axis=0, concat_axis=0, tiled=True)
    if tensor_count == 1:
        summed = project(arrived, down_weight).astype(jnp.bfloat16)
    else:
        partial_rows = project(arrived, down_weight).astype(jnp.bfloat16)
        outbound = lax.dynamic_slice_in_dim(partial_rows, other * width_half, width_half, 3)
        mine = lax.dynamic_slice_in_dim(partial_rows, position * width_half, width_half, 3)
        inbound = passed_along(outbound, "tensor", 1)
        summed = (mine.astype(jnp.float32) + inbound.astype(jnp.float32)).astype(jnp.bfloat16)
    returned = lax.all_to_all(summed, "expert", split_axis=0, concat_axis=0, tiled=True)
    flat_back = returned.reshape(all_experts * capacity, returned.shape[3])
    picked = (
        flat_back[slots].astype(jnp.float32).reshape(token_count, choose_count, returned.shape[3])
    )
    combined = jnp.sum(picked * gate_weights[:, :, None], axis=1)
    return combined.astype(jnp.bfloat16)


def spread_kernel(relatives, own_ref, ids_ref, gates_ref, hidden_ref, *refs):
    out_refs = refs[-len(relatives) :]
    own = own_ref[0]
    choose_count, token_count = ids_ref.shape
    shape = (token_count, token_count * choose_count)
    row = lax.broadcasted_iota(jnp.int32, shape, 0) * choose_count
    column = lax.broadcasted_iota(jnp.int32, shape, 1)
    same = (column >= row) & (column < row + choose_count)
    across = (choose_count, token_count * choose_count)
    choice = lax.rem(lax.broadcasted_iota(jnp.int32, across, 1), choose_count)
    repeat = (choice == lax.broadcasted_iota(jnp.int32, across, 0)).astype(jnp.float32)
    ids, gate_weights = ids_ref[...].T, gates_ref[...].T
    spread_ids = jnp.dot(ids.astype(jnp.float32), repeat, preferred_element_type=jnp.float32)
    own_row = jnp.where(same, (spread_ids + 0.5).astype(jnp.int32), -1)
    for at in range(0, len(relatives), 2):
        picks, gates = [], []
        for relative in relatives[at : at + 2]:
            for core in range(2):
                expert = own ^ (2 * relative + core)
                picks.append((own_row == expert).astype(jnp.float32).astype(hidden_ref.dtype))
                gates.append(
                    jnp.sum(jnp.where(ids == expert, gate_weights, 0.0), axis=1, keepdims=True)
                )
        rows = jnp.dot(
            jnp.concatenate(picks, axis=0), hidden_ref[...], preferred_element_type=jnp.float32
        )
        scaled = (rows * jnp.concatenate(gates, axis=0)).astype(hidden_ref.dtype)
        for place in range(len(picks) // 2):
            block = scaled[2 * place * token_count : 2 * (place + 1) * token_count]
            out_refs[at + place][...] = block.reshape(2, token_count, -1)


def spread_rows(hidden, expert_ids, gate_weights, own, relatives, held=None):
    token_count, choose_count, width = hidden.shape
    vmem = pl.BlockSpec(memory_space=pltpu.VMEM)
    block = jax.ShapeDtypeStruct((2, token_count, width), hidden.dtype)
    more = [] if held is None else [held]
    return pl.pallas_call(
        functools.partial(spread_kernel, relatives),
        in_specs=[pl.BlockSpec(memory_space=pltpu.SMEM)] + [vmem] * (3 + len(more)),
        out_specs=[vmem] * len(relatives),
        out_shape=[block] * len(relatives),
        compiler_params=pltpu.CompilerParams(vmem_limit_bytes=24 << 20),
        cost_estimate=pl.CostEstimate(flops=0, bytes_accessed=0, transcendentals=0),
        name="spread_rows",
    )(
        own.reshape(1),
        expert_ids.T,
        gate_weights.T,
        hidden.reshape(token_count * choose_count, width),
        *more,
    )


def mix_kernel(*refs):
    rows, (near_ref, far_ref, out_ref, joined_ref) = refs[:-4], refs[-4:]
    tokens = rows[0].shape[1]

    @pl.when(pl.program_id(0) == 0)
    def _():
        for place, ref in enumerate(rows):
            joined_ref[:, place * tokens : (place + 1) * tokens] = ref[...]

    total = jnp.dot(joined_ref[0], near_ref[...], preferred_element_type=jnp.float32)
    total += jnp.dot(joined_ref[1], far_ref[...], preferred_element_type=jnp.float32)
    out_ref[...] = total.reshape(len(rows), tokens, -1).astype(out_ref.dtype)


def mix(rows, near, far, start, width, weight_of_cost):
    _, tokens, depth = rows[0].shape
    whole = pl.BlockSpec((2, tokens, depth), lambda i: (0, 0, 0))
    weight = pl.BlockSpec((depth, TILE), lambda i: (0, start // TILE + i))
    return pl.pallas_call(
        mix_kernel,
        grid=(width // TILE,),
        in_specs=[whole] * len(rows) + [weight] * 2,
        out_specs=pl.BlockSpec((len(rows), tokens, TILE), lambda i: (0, 0, i)),
        out_shape=jax.ShapeDtypeStruct((len(rows), tokens, width), jnp.bfloat16),
        scratch_shapes=[pltpu.VMEM((2, len(rows) * tokens, depth), jnp.bfloat16)],
        compiler_params=pltpu.CompilerParams(vmem_limit_bytes=24 << 20),
        cost_estimate=pl.CostEstimate(
            flops=int(weight_of_cost * 4 * len(rows) * tokens * depth * width),
            bytes_accessed=int(weight_of_cost * 4 * depth * width),
            transcendentals=0,
        ),
        name="mix",
    )(*rows, near, far)


def swap(block, axis, distance):
    return lax.ppermute(block, axis, [(i, i ^ distance) for i in range(lax.axis_size(axis))])


def send_to_chip(block, relative):
    sizes = (lax.axis_size("z"), lax.axis_size("x"))
    return lax.ppermute(
        block, ("z", "x"), [(i, i ^ relative) for i in range(sizes[0] * sizes[1])]
    )


def after(value, earlier):
    return lax.optimization_barrier((value, earlier))[0]


def dense_body(hidden, expert_ids, gate_weights, down_weight):
    own = (lax.axis_index("z") * 2 + lax.axis_index("x")) * 2 + lax.axis_index("core")
    near = down_weight[0]
    far = swap(near, "core", 1)
    odd, even = (7, 5, 3, 1), (6, 4, 2, 0)
    arrived = [None] * CHIPS
    blocks = spread_rows(hidden, expert_ids, gate_weights, own, odd)
    for relative, block in zip(odd, blocks):
        arrived[relative] = send_to_chip(block, relative)
    blocks = spread_rows(hidden, expert_ids, gate_weights, own, even, near)
    blocks = after(blocks, [arrived[r] for r in odd])
    for relative, block in zip(even, blocks):
        arrived[relative] = send_to_chip(block, relative) if relative else block
    given, kept, lines, pairs, results = [], [], [], [], []

    def mix_odd(i, earlier):
        arrived[7] = after(arrived[7], earlier)
        block = mix([arrived[r] for r in odd], near, far, *COLUMNS[i], LIGHT)
        given.append(block)
        return block

    def mix_even(parts, earlier, weight):
        start, width = COLUMNS[parts[0]][0], sum(COLUMNS[i][1] for i in parts)
        arrived[0] = after(arrived[0], earlier)
        block = mix([arrived[r] for r in even], near, far, start, width, weight)
        for i in parts:
            low = COLUMNS[i][0] - start
            kept.append(block[:, :, low : low + COLUMNS[i][1]])
        return block

    def add_x(i, earlier):
        line = after(kept[i], earlier).astype(jnp.float32) + across[i].astype(jnp.float32)
        lines.append((line[1::2], swap(line[0::2].astype(jnp.bfloat16), "z", 1)))
        return line

    def add_z(i, earlier):
        pair = after(lines[i][0], earlier) + lines[i][1].astype(jnp.float32)
        pairs.append((pair[1], swap(pair[0].astype(jnp.bfloat16), "z", 2)))
        return pair

    last = blocks[-1]
    for i in range(len(COLUMNS)):
        last = mix_odd(i, last)
    across = [swap(block, "x", 1) for block in given]
    last = mix_even((0,), last, HEAVY)
    last = add_x(0, last)
    last = mix_even((1,), last, LIGHT)
    last = mix_even((2,), last, LIGHT)
    last = add_x(1, last)
    last = add_z(0, last)
    last = add_x(2, last)
    last = add_z(1, last)
    add_z(2, last)
    for mine, theirs in pairs:
        results.append((mine + theirs.astype(jnp.float32)).astype(jnp.bfloat16))
    return jnp.concatenate(results, axis=1)


def solution(mesh):
    groups, owners, tensors = (mesh.shape[axis] for axis in ("groups", "expert", "tensor"))

    def whole(hidden, expert_ids, gate_weights, down_weight):
        tokens = hidden.shape[0] // (groups * owners)
        capacity = 2 * tokens * hidden.shape[1] // down_weight.shape[0]
        one_each = owners == 2 * CHIPS and down_weight.shape[0] == owners
        if tensors == 1 and one_each and capacity >= tokens:
            axes = ("groups", "z", "x", "core")
            used = Mesh(mesh.devices.reshape(groups, CHIPS // 2, 2, 2), axes)
            run, batch = dense_body, P(axes)
            weight, out = P(axes[1:]), P(axes)
        else:
            used, run, batch = mesh, slotted_body, P(("groups", "expert"))
            weight = P("expert", "tensor", None)
            out = P(("groups", "expert"), "tensor")
        rows = batch if tensors == 1 else P(("groups", "expert"), None, "tensor")
        return jax.shard_map(
            run,
            mesh=used,
            in_specs=(rows, batch, batch, weight),
            out_specs=out,
            check_vma=False,
        )(hidden, expert_ids, gate_weights, down_weight)

    return whole
```

```python
import functools

import jax
import jax.numpy as jnp
from jax import lax
from jax.experimental import pallas as pl
from jax.experimental.pallas import tpu as pltpu
from jax.sharding import Mesh, PartitionSpec as P

CHIPS = 8
TILE = 512
COLUMNS = ((0, 1536), (1536, 1536), (3072, 512))
LIGHT = 0.01


def passed_along(block, axis, distance):
    devices = range(lax.axis_size(axis))
    route = [((i - distance) % len(devices), i) for i in devices]
    return lax.ppermute(block, axis, route)


def project(arrived, weights):
    return jnp.einsum("secf,efd->secd", arrived, weights, preferred_element_type=jnp.float32)


def slotted_body(hidden, expert_ids, gate_weights, down_weight):
    token_count, choose_count, half_hidden = hidden.shape
    local_experts = down_weight.shape[0]
    owner_count = lax.axis_size("expert")
    tensor_count = lax.axis_size("tensor")
    all_experts = owner_count * local_experts
    capacity = min(token_count, max(2, 2 * token_count * choose_count // all_experts))
    flat_ids = expert_ids.reshape(-1)
    onehot = (flat_ids[:, None] == jnp.arange(all_experts, dtype=jnp.int32)[None, :]).astype(
        jnp.int32
    )
    running = jnp.cumsum(onehot, axis=0)
    ranks = jnp.sum(onehot * running, axis=1) - 1
    slots = flat_ids * capacity + ranks
    copy_rows = hidden.reshape(token_count * choose_count, half_hidden)
    outgoing = (
        jnp.zeros((all_experts * capacity, half_hidden), hidden.dtype).at[slots].set(copy_rows)
    )
    outgoing = outgoing.reshape(owner_count, local_experts, capacity, half_hidden)
    width_total = down_weight.shape[2]
    width_half = width_total // tensor_count
    position = lax.axis_index("tensor")
    other = 1 - position
    arrived = lax.all_to_all(outgoing, "expert", split_axis=0, concat_axis=0, tiled=True)
    if tensor_count == 1:
        summed = project(arrived, down_weight).astype(jnp.bfloat16)
    else:
        partial_rows = project(arrived, down_weight).astype(jnp.bfloat16)
        outbound = lax.dynamic_slice_in_dim(partial_rows, other * width_half, width_half, 3)
        mine = lax.dynamic_slice_in_dim(partial_rows, position * width_half, width_half, 3)
        inbound = passed_along(outbound, "tensor", 1)
        summed = (mine.astype(jnp.float32) + inbound.astype(jnp.float32)).astype(jnp.bfloat16)
    returned = lax.all_to_all(summed, "expert", split_axis=0, concat_axis=0, tiled=True)
    flat_back = returned.reshape(all_experts * capacity, returned.shape[3])
    picked = (
        flat_back[slots].astype(jnp.float32).reshape(token_count, choose_count, returned.shape[3])
    )
    combined = jnp.sum(picked * gate_weights[:, :, None], axis=1)
    return combined.astype(jnp.bfloat16)


def fetching_kernel(relatives, own_ref, ids_hbm, gates_hbm, hidden_hbm, *refs):
    out_refs, fetched, sems = refs[: len(relatives)], refs[len(relatives) : -1], refs[-1]
    copies = [
        pltpu.make_async_copy(source, target, sems.at[i])
        for i, (source, target) in enumerate(zip((ids_hbm, gates_hbm, hidden_hbm), fetched))
    ]
    for copy in copies:
        copy.start()
    for copy in copies:
        copy.wait()
    spread_kernel(relatives, own_ref, *fetched, *out_refs)


def spread_kernel(relatives, own_ref, ids_ref, gates_ref, hidden_ref, *refs):
    out_refs = refs[-len(relatives) :]
    own = own_ref[0]
    choose_count, token_count = ids_ref.shape
    shape = (token_count, token_count * choose_count)
    row = lax.broadcasted_iota(jnp.int32, shape, 0) * choose_count
    column = lax.broadcasted_iota(jnp.int32, shape, 1)
    same = (column >= row) & (column < row + choose_count)
    across = (choose_count, token_count * choose_count)
    choice = lax.rem(lax.broadcasted_iota(jnp.int32, across, 1), choose_count)
    repeat = (choice == lax.broadcasted_iota(jnp.int32, across, 0)).astype(jnp.float32)
    ids, gate_weights = ids_ref[...].T, gates_ref[...].T
    spread_ids = jnp.dot(ids.astype(jnp.float32), repeat, preferred_element_type=jnp.float32)
    own_row = jnp.where(same, (spread_ids + 0.5).astype(jnp.int32), -1)
    for at in range(0, len(relatives), 2):
        picks, gates = [], []
        for relative in relatives[at : at + 2]:
            for core in range(2):
                expert = own ^ (2 * relative + core)
                picks.append((own_row == expert).astype(jnp.float32).astype(hidden_ref.dtype))
                gates.append(
                    jnp.sum(jnp.where(ids == expert, gate_weights, 0.0), axis=1, keepdims=True)
                )
        rows = jnp.dot(
            jnp.concatenate(picks, axis=0), hidden_ref[...], preferred_element_type=jnp.float32
        )
        scaled = (rows * jnp.concatenate(gates, axis=0)).astype(hidden_ref.dtype)
        for place in range(len(picks) // 2):
            block = scaled[2 * place * token_count : 2 * (place + 1) * token_count]
            out_refs[at + place][...] = block.reshape(2, token_count, -1)


def spread_rows(hidden, expert_ids, gate_weights, own, relatives, held=None):
    token_count, choose_count, width = hidden.shape
    rows = token_count * choose_count
    vmem = pl.BlockSpec(memory_space=pltpu.VMEM)
    block = jax.ShapeDtypeStruct((2, token_count, width), hidden.dtype)
    more = [] if held is None else [held]
    scratch = [] if more else [
        pltpu.VMEM((choose_count, token_count), expert_ids.dtype),
        pltpu.VMEM((choose_count, token_count), gate_weights.dtype),
        pltpu.VMEM((rows, width), hidden.dtype),
        pltpu.SemaphoreType.DMA((3,)),
    ]
    given = vmem if more else pl.BlockSpec(memory_space=pl.ANY)
    return pl.pallas_call(
        functools.partial(spread_kernel if more else fetching_kernel, relatives),
        in_specs=[pl.BlockSpec(memory_space=pltpu.SMEM)] + [given] * 3 + [vmem] * len(more),
        out_specs=[vmem] * len(relatives),
        out_shape=[block] * len(relatives),
        scratch_shapes=scratch,
        compiler_params=pltpu.CompilerParams(vmem_limit_bytes=(24 if more else 56) << 20),
        cost_estimate=pl.CostEstimate(flops=0, bytes_accessed=0, transcendentals=0),
        name="spread_rows",
    )(
        own.reshape(1),
        expert_ids.T,
        gate_weights.T,
        hidden.reshape(rows, width),
        *more,
    )


def mix_kernel(*refs):
    rows, (near_ref, far_ref, out_ref, joined_ref) = refs[:-4], refs[-4:]
    tokens = rows[0].shape[1]

    @pl.when(pl.program_id(0) == 0)
    def _():
        for place, ref in enumerate(rows):
            joined_ref[:, place * tokens : (place + 1) * tokens] = ref[...]

    total = jnp.dot(joined_ref[0], near_ref[...], preferred_element_type=jnp.float32)
    total += jnp.dot(joined_ref[1], far_ref[...], preferred_element_type=jnp.float32)
    out_ref[...] = total.reshape(len(rows), tokens, -1).astype(out_ref.dtype)


def mix(rows, near, far, start, width, weight_of_cost):
    _, tokens, depth = rows[0].shape
    whole = pl.BlockSpec((2, tokens, depth), lambda i: (0, 0, 0))
    weight = pl.BlockSpec((depth, TILE), lambda i: (0, start // TILE + i))
    return pl.pallas_call(
        mix_kernel,
        grid=(width // TILE,),
        in_specs=[whole] * len(rows) + [weight] * 2,
        out_specs=pl.BlockSpec((len(rows), tokens, TILE), lambda i: (0, 0, i)),
        out_shape=jax.ShapeDtypeStruct((len(rows), tokens, width), jnp.bfloat16),
        scratch_shapes=[pltpu.VMEM((2, len(rows) * tokens, depth), jnp.bfloat16)],
        compiler_params=pltpu.CompilerParams(vmem_limit_bytes=24 << 20),
        cost_estimate=pl.CostEstimate(
            flops=int(weight_of_cost * 4 * len(rows) * tokens * depth * width),
            bytes_accessed=int(weight_of_cost * 4 * depth * width),
            transcendentals=0,
        ),
        name="mix",
    )(*rows, near, far)


def swap(block, axis, distance):
    return lax.ppermute(block, axis, [(i, i ^ distance) for i in range(lax.axis_size(axis))])


def send_to_chip(block, relative):
    sizes = (lax.axis_size("z"), lax.axis_size("x"))
    return lax.ppermute(
        block, ("z", "x"), [(i, i ^ relative) for i in range(sizes[0] * sizes[1])]
    )


def after(value, earlier):
    return lax.optimization_barrier((value, earlier))[0]


def dense_body(hidden, expert_ids, gate_weights, down_weight):
    own = (lax.axis_index("z") * 2 + lax.axis_index("x")) * 2 + lax.axis_index("core")
    near = down_weight[0]
    far = swap(near, "core", 1)
    odd, even = (7, 5, 3, 1), (6, 4, 2, 0)
    arrived = [None] * CHIPS
    blocks = spread_rows(hidden, expert_ids, gate_weights, own, odd)
    for relative, block in zip(odd, blocks):
        arrived[relative] = send_to_chip(block, relative)
    blocks = spread_rows(hidden, expert_ids, gate_weights, own, even, near)
    blocks = after(blocks, [arrived[r] for r in odd])
    for relative, block in zip(even, blocks):
        arrived[relative] = send_to_chip(block, relative) if relative else block
    given, kept, lines, pairs, results = [], [], [], [], []

    def mix_odd(i, earlier):
        arrived[7] = after(arrived[7], earlier)
        block = mix([arrived[r] for r in odd], near, far, *COLUMNS[i], LIGHT)
        given.append(block)
        return block

    def mix_even(parts, earlier, weight):
        start, width = COLUMNS[parts[0]][0], sum(COLUMNS[i][1] for i in parts)
        arrived[0] = after(arrived[0], earlier)
        block = mix([arrived[r] for r in even], near, far, start, width, weight)
        for i in parts:
            low = COLUMNS[i][0] - start
            kept.append(block[:, :, low : low + COLUMNS[i][1]])
        return block

    def add_x(i, earlier, parts=1):
        line = after(kept[i], earlier).astype(jnp.float32) + across[i].astype(jnp.float32)
        for part in jnp.split(line, parts, axis=2):
            lines.append((part[1::2], swap(part[0::2].astype(jnp.bfloat16), "z", 1)))
        return line

    def add_z(i, earlier):
        pair = after(lines[i][0], earlier) + lines[i][1].astype(jnp.float32)
        pairs.append((pair[1], swap(pair[0].astype(jnp.bfloat16), "z", 2)))
        return pair

    last = blocks[-1]
    for i in range(len(COLUMNS)):
        last = mix_odd(i, last)
    across = [swap(block, "x", 1) for block in given]
    last = mix_even((0,), last, LIGHT)
    last = add_x(0, last)
    last = mix_even((1,), last, LIGHT)
    last = mix_even((2,), last, LIGHT)
    last = add_x(1, last, 2)
    last = add_z(0, last)
    last = add_x(2, last)
    for i in range(1, 4):
        last = add_z(i, last)
    for mine, theirs in pairs:
        results.append((mine + theirs.astype(jnp.float32)).astype(jnp.bfloat16))
    return jnp.concatenate(results, axis=1)


def solution(mesh):
    groups, owners, tensors = (mesh.shape[axis] for axis in ("groups", "expert", "tensor"))

    def whole(hidden, expert_ids, gate_weights, down_weight):
        tokens = hidden.shape[0] // (groups * owners)
        capacity = 2 * tokens * hidden.shape[1] // down_weight.shape[0]
        one_each = owners == 2 * CHIPS and down_weight.shape[0] == owners
        if tensors == 1 and one_each and capacity >= tokens:
            axes = ("groups", "z", "x", "core")
            used = Mesh(mesh.devices.reshape(groups, CHIPS // 2, 2, 2), axes)
            run, batch = dense_body, P(axes)
            weight, out = P(axes[1:]), P(axes)
        else:
            used, run, batch = mesh, slotted_body, P(("groups", "expert"))
            weight = P("expert", "tensor", None)
            out = P(("groups", "expert"), "tensor")
        rows = batch if tensors == 1 else P(("groups", "expert"), None, "tensor")
        return jax.shard_map(
            run,
            mesh=used,
            in_specs=(rows, batch, batch, weight),
            out_specs=out,
            check_vma=False,
        )(hidden, expert_ids, gate_weights, down_weight)

    return whole
```

```python
import functools

import jax
import jax.numpy as jnp
from jax import lax
from jax.experimental import pallas as pl
from jax.experimental.pallas import tpu as pltpu
from jax.sharding import Mesh, PartitionSpec as P

CHIPS = 8
TILE = 512
COLUMNS = ((0, 1024), (1024, 1024), (2048, 1536))
LIGHT = 0.01


def passed_along(block, axis, distance):
    devices = range(lax.axis_size(axis))
    route = [((i - distance) % len(devices), i) for i in devices]
    return lax.ppermute(block, axis, route)


def project(arrived, weights):
    return jnp.einsum("secf,efd->secd", arrived, weights, preferred_element_type=jnp.float32)


def slotted_body(hidden, expert_ids, gate_weights, down_weight):
    token_count, choose_count, half_hidden = hidden.shape
    local_experts = down_weight.shape[0]
    owner_count = lax.axis_size("expert")
    tensor_count = lax.axis_size("tensor")
    all_experts = owner_count * local_experts
    capacity = min(token_count, max(2, 2 * token_count * choose_count // all_experts))
    flat_ids = expert_ids.reshape(-1)
    onehot = (flat_ids[:, None] == jnp.arange(all_experts, dtype=jnp.int32)[None, :]).astype(
        jnp.int32
    )
    running = jnp.cumsum(onehot, axis=0)
    ranks = jnp.sum(onehot * running, axis=1) - 1
    slots = flat_ids * capacity + ranks
    copy_rows = hidden.reshape(token_count * choose_count, half_hidden)
    outgoing = (
        jnp.zeros((all_experts * capacity, half_hidden), hidden.dtype).at[slots].set(copy_rows)
    )
    outgoing = outgoing.reshape(owner_count, local_experts, capacity, half_hidden)
    width_total = down_weight.shape[2]
    width_half = width_total // tensor_count
    position = lax.axis_index("tensor")
    other = 1 - position
    arrived = lax.all_to_all(outgoing, "expert", split_axis=0, concat_axis=0, tiled=True)
    if tensor_count == 1:
        summed = project(arrived, down_weight).astype(jnp.bfloat16)
    else:
        partial_rows = project(arrived, down_weight).astype(jnp.bfloat16)
        outbound = lax.dynamic_slice_in_dim(partial_rows, other * width_half, width_half, 3)
        mine = lax.dynamic_slice_in_dim(partial_rows, position * width_half, width_half, 3)
        inbound = passed_along(outbound, "tensor", 1)
        summed = (mine.astype(jnp.float32) + inbound.astype(jnp.float32)).astype(jnp.bfloat16)
    returned = lax.all_to_all(summed, "expert", split_axis=0, concat_axis=0, tiled=True)
    flat_back = returned.reshape(all_experts * capacity, returned.shape[3])
    picked = (
        flat_back[slots].astype(jnp.float32).reshape(token_count, choose_count, returned.shape[3])
    )
    combined = jnp.sum(picked * gate_weights[:, :, None], axis=1)
    return combined.astype(jnp.bfloat16)


def fetching_kernel(relatives, own_ref, ids_hbm, gates_hbm, hidden_hbm, *refs):
    out_refs, fetched, sems = refs[: len(relatives)], refs[len(relatives) : -1], refs[-1]
    copies = [
        pltpu.make_async_copy(source, target, sems.at[i])
        for i, (source, target) in enumerate(zip((ids_hbm, gates_hbm, hidden_hbm), fetched))
    ]
    for copy in copies:
        copy.start()
    for copy in copies:
        copy.wait()
    spread_kernel(relatives, own_ref, *fetched, *out_refs)


def spread_kernel(relatives, own_ref, ids_ref, gates_ref, hidden_ref, *refs):
    out_refs = refs[-len(relatives) :]
    own = own_ref[0]
    choose_count, token_count = ids_ref.shape
    shape = (token_count, token_count * choose_count)
    row = lax.broadcasted_iota(jnp.int32, shape, 0) * choose_count
    column = lax.broadcasted_iota(jnp.int32, shape, 1)
    same = (column >= row) & (column < row + choose_count)
    across = (choose_count, token_count * choose_count)
    choice = lax.rem(lax.broadcasted_iota(jnp.int32, across, 1), choose_count)
    repeat = (choice == lax.broadcasted_iota(jnp.int32, across, 0)).astype(jnp.float32)
    ids, gate_weights = ids_ref[...].T, gates_ref[...].T
    spread_ids = jnp.dot(ids.astype(jnp.float32), repeat, preferred_element_type=jnp.float32)
    own_row = jnp.where(same, (spread_ids + 0.5).astype(jnp.int32), -1)
    for at in range(0, len(relatives), 2):
        picks, gates = [], []
        for relative in relatives[at : at + 2]:
            for core in range(2):
                expert = own ^ (2 * relative + core)
                picks.append((own_row == expert).astype(jnp.float32).astype(hidden_ref.dtype))
                gates.append(
                    jnp.sum(jnp.where(ids == expert, gate_weights, 0.0), axis=1, keepdims=True)
                )
        rows = jnp.dot(
            jnp.concatenate(picks, axis=0), hidden_ref[...], preferred_element_type=jnp.float32
        )
        scaled = (rows * jnp.concatenate(gates, axis=0)).astype(hidden_ref.dtype)
        for place in range(len(picks) // 2):
            block = scaled[2 * place * token_count : 2 * (place + 1) * token_count]
            out_refs[at + place][...] = block.reshape(2, token_count, -1)


def spread_rows(hidden, expert_ids, gate_weights, own, relatives, held=None):
    token_count, choose_count, width = hidden.shape
    rows = token_count * choose_count
    vmem = pl.BlockSpec(memory_space=pltpu.VMEM)
    block = jax.ShapeDtypeStruct((2, token_count, width), hidden.dtype)
    more = [] if held is None else [held]
    scratch = [] if more else [
        pltpu.VMEM((choose_count, token_count), expert_ids.dtype),
        pltpu.VMEM((choose_count, token_count), gate_weights.dtype),
        pltpu.VMEM((rows, width), hidden.dtype),
        pltpu.SemaphoreType.DMA((3,)),
    ]
    given = vmem if more else pl.BlockSpec(memory_space=pl.ANY)
    return pl.pallas_call(
        functools.partial(spread_kernel if more else fetching_kernel, relatives),
        in_specs=[pl.BlockSpec(memory_space=pltpu.SMEM)] + [given] * 3 + [vmem] * len(more),
        out_specs=[vmem] * len(relatives),
        out_shape=[block] * len(relatives),
        scratch_shapes=scratch,
        compiler_params=pltpu.CompilerParams(vmem_limit_bytes=(24 if more else 56) << 20),
        cost_estimate=pl.CostEstimate(flops=0, bytes_accessed=0, transcendentals=0),
        name="spread_rows",
    )(
        own.reshape(1),
        expert_ids.T,
        gate_weights.T,
        hidden.reshape(rows, width),
        *more,
    )


def mix_kernel(*refs):
    rows, (near_ref, far_ref, out_ref, joined_ref) = refs[:-4], refs[-4:]
    tokens = rows[0].shape[1]

    @pl.when(pl.program_id(0) == 0)
    def _():
        for place, ref in enumerate(rows):
            joined_ref[:, place * tokens : (place + 1) * tokens] = ref[...]

    total = jnp.dot(joined_ref[0], near_ref[...], preferred_element_type=jnp.float32)
    total += jnp.dot(joined_ref[1], far_ref[...], preferred_element_type=jnp.float32)
    out_ref[...] = total.reshape(len(rows), tokens, -1).astype(out_ref.dtype)


def mix(rows, near, far, start, width, weight_of_cost):
    _, tokens, depth = rows[0].shape
    whole = pl.BlockSpec((2, tokens, depth), lambda i: (0, 0, 0))
    weight = pl.BlockSpec((depth, TILE), lambda i: (0, start // TILE + i))
    return pl.pallas_call(
        mix_kernel,
        grid=(width // TILE,),
        in_specs=[whole] * len(rows) + [weight] * 2,
        out_specs=pl.BlockSpec((len(rows), tokens, TILE), lambda i: (0, 0, i)),
        out_shape=jax.ShapeDtypeStruct((len(rows), tokens, width), jnp.bfloat16),
        scratch_shapes=[pltpu.VMEM((2, len(rows) * tokens, depth), jnp.bfloat16)],
        compiler_params=pltpu.CompilerParams(vmem_limit_bytes=24 << 20),
        cost_estimate=pl.CostEstimate(
            flops=int(weight_of_cost * 4 * len(rows) * tokens * depth * width),
            bytes_accessed=int(weight_of_cost * 4 * depth * width),
            transcendentals=0,
        ),
        name="mix",
    )(*rows, near, far)


def swap(block, axis, distance):
    return lax.ppermute(block, axis, [(i, i ^ distance) for i in range(lax.axis_size(axis))])


def send_to_chip(block, relative):
    sizes = (lax.axis_size("z"), lax.axis_size("x"))
    return lax.ppermute(
        block, ("z", "x"), [(i, i ^ relative) for i in range(sizes[0] * sizes[1])]
    )


def after(value, earlier):
    return lax.optimization_barrier((value, earlier))[0]


def dense_body(hidden, expert_ids, gate_weights, down_weight):
    own = (lax.axis_index("z") * 2 + lax.axis_index("x")) * 2 + lax.axis_index("core")
    near = down_weight[0]
    far = swap(near, "core", 1)
    odd, even = (7, 5, 3, 1), (6, 4, 2, 0)
    arrived = [None] * CHIPS
    blocks = spread_rows(hidden, expert_ids, gate_weights, own, odd)
    for relative, block in zip(odd, blocks):
        arrived[relative] = send_to_chip(block, relative)
    blocks = spread_rows(hidden, expert_ids, gate_weights, own, even, near)
    blocks = after(blocks, [arrived[r] for r in odd])
    for relative, block in zip(even, blocks):
        arrived[relative] = send_to_chip(block, relative) if relative else block
    given, kept, lines, pairs, results = [], [], [], [], []

    def mix_odd(i, earlier):
        arrived[7] = after(arrived[7], earlier)
        block = mix([arrived[r] for r in odd], near, far, *COLUMNS[i], LIGHT)
        given.append(block)
        return block

    def mix_even(parts, earlier, weight):
        start, width = COLUMNS[parts[0]][0], sum(COLUMNS[i][1] for i in parts)
        arrived[0] = after(arrived[0], earlier)
        block = mix([arrived[r] for r in even], near, far, start, width, weight)
        for i in parts:
            low = COLUMNS[i][0] - start
            kept.append(block[:, :, low : low + COLUMNS[i][1]])
        return block

    def add_x(i, earlier):
        line = after(kept[i], earlier).astype(jnp.float32) + across[i].astype(jnp.float32)
        lines.append((line[1::2], swap(line[0::2].astype(jnp.bfloat16), "z", 1)))
        return line

    def add_z(i, earlier):
        pair = after(lines[i][0], earlier) + lines[i][1].astype(jnp.float32)
        pairs.append((pair[1], swap(pair[0].astype(jnp.bfloat16), "z", 2)))
        return pair

    last = blocks[-1]
    for i in range(len(COLUMNS)):
        last = mix_odd(i, last)
    across = [swap(block, "x", 1) for block in given]
    last = mix_even((0,), last, LIGHT)
    last = add_x(0, last)
    last = mix_even((1,), last, LIGHT)
    last = mix_even((2,), last, LIGHT)
    last = add_x(1, last)
    last = add_z(0, last)
    last = add_x(2, last)
    last = add_z(1, last)
    add_z(2, last)
    for mine, theirs in pairs:
        results.append((mine + theirs.astype(jnp.float32)).astype(jnp.bfloat16))
    return jnp.concatenate(results, axis=1)


def solution(mesh):
    groups, owners, tensors = (mesh.shape[axis] for axis in ("groups", "expert", "tensor"))

    def whole(hidden, expert_ids, gate_weights, down_weight):
        tokens = hidden.shape[0] // (groups * owners)
        capacity = 2 * tokens * hidden.shape[1] // down_weight.shape[0]
        one_each = owners == 2 * CHIPS and down_weight.shape[0] == owners
        if tensors == 1 and one_each and capacity >= tokens:
            axes = ("groups", "z", "x", "core")
            used = Mesh(mesh.devices.reshape(groups, CHIPS // 2, 2, 2), axes)
            run, batch = dense_body, P(axes)
            weight, out = P(axes[1:]), P(axes)
        else:
            used, run, batch = mesh, slotted_body, P(("groups", "expert"))
            weight = P("expert", "tensor", None)
            out = P(("groups", "expert"), "tensor")
        rows = batch if tensors == 1 else P(("groups", "expert"), None, "tensor")
        return jax.shard_map(
            run,
            mesh=used,
            in_specs=(rows, batch, batch, weight),
            out_specs=out,
            check_vma=False,
        )(hidden, expert_ids, gate_weights, down_weight)

    return whole
```

```python
import functools

import jax
import jax.numpy as jnp
from jax import lax
from jax.experimental import pallas as pl
from jax.experimental.pallas import tpu as pltpu
from jax.sharding import Mesh, PartitionSpec as P

CHIPS = 8
TILE = 512
COLUMNS = ((0, 1024), (1024, 1024), (2048, 1536))
LIGHT = 0.01


def passed_along(block, axis, distance):
    devices = range(lax.axis_size(axis))
    route = [((i - distance) % len(devices), i) for i in devices]
    return lax.ppermute(block, axis, route)


def project(arrived, weights):
    return jnp.einsum("secf,efd->secd", arrived, weights, preferred_element_type=jnp.float32)


def slotted_body(hidden, expert_ids, gate_weights, down_weight):
    token_count, choose_count, half_hidden = hidden.shape
    local_experts = down_weight.shape[0]
    owner_count = lax.axis_size("expert")
    tensor_count = lax.axis_size("tensor")
    all_experts = owner_count * local_experts
    capacity = min(token_count, max(2, 2 * token_count * choose_count // all_experts))
    flat_ids = expert_ids.reshape(-1)
    onehot = (flat_ids[:, None] == jnp.arange(all_experts, dtype=jnp.int32)[None, :]).astype(
        jnp.int32
    )
    running = jnp.cumsum(onehot, axis=0)
    ranks = jnp.sum(onehot * running, axis=1) - 1
    slots = flat_ids * capacity + ranks
    copy_rows = hidden.reshape(token_count * choose_count, half_hidden)
    outgoing = (
        jnp.zeros((all_experts * capacity, half_hidden), hidden.dtype).at[slots].set(copy_rows)
    )
    outgoing = outgoing.reshape(owner_count, local_experts, capacity, half_hidden)
    width_total = down_weight.shape[2]
    width_half = width_total // tensor_count
    position = lax.axis_index("tensor")
    other = 1 - position
    arrived = lax.all_to_all(outgoing, "expert", split_axis=0, concat_axis=0, tiled=True)
    if tensor_count == 1:
        summed = project(arrived, down_weight).astype(jnp.bfloat16)
    else:
        partial_rows = project(arrived, down_weight).astype(jnp.bfloat16)
        outbound = lax.dynamic_slice_in_dim(partial_rows, other * width_half, width_half, 3)
        mine = lax.dynamic_slice_in_dim(partial_rows, position * width_half, width_half, 3)
        inbound = passed_along(outbound, "tensor", 1)
        summed = (mine.astype(jnp.float32) + inbound.astype(jnp.float32)).astype(jnp.bfloat16)
    returned = lax.all_to_all(summed, "expert", split_axis=0, concat_axis=0, tiled=True)
    flat_back = returned.reshape(all_experts * capacity, returned.shape[3])
    picked = (
        flat_back[slots].astype(jnp.float32).reshape(token_count, choose_count, returned.shape[3])
    )
    combined = jnp.sum(picked * gate_weights[:, :, None], axis=1)
    return combined.astype(jnp.bfloat16)


def fetching_kernel(relatives, own_ref, ids_hbm, gates_hbm, hidden_hbm, *refs):
    out_refs, fetched, sems = refs[: len(relatives)], refs[len(relatives) : -1], refs[-1]
    copies = [
        pltpu.make_async_copy(source, target, sems.at[i])
        for i, (source, target) in enumerate(zip((ids_hbm, gates_hbm, hidden_hbm), fetched))
    ]
    for copy in copies:
        copy.start()
    for copy in copies:
        copy.wait()
    spread_kernel(relatives, own_ref, *fetched, *out_refs)


def spread_kernel(relatives, own_ref, ids_ref, gates_ref, hidden_ref, *refs):
    out_refs = refs[-len(relatives) :]
    own = own_ref[0]
    choose_count, token_count = ids_ref.shape
    shape = (token_count, token_count * choose_count)
    row = lax.broadcasted_iota(jnp.int32, shape, 0) * choose_count
    column = lax.broadcasted_iota(jnp.int32, shape, 1)
    same = (column >= row) & (column < row + choose_count)
    across = (choose_count, token_count * choose_count)
    choice = lax.rem(lax.broadcasted_iota(jnp.int32, across, 1), choose_count)
    repeat = (choice == lax.broadcasted_iota(jnp.int32, across, 0)).astype(jnp.float32)
    ids, gate_weights = ids_ref[...].T, gates_ref[...].T
    spread_ids = jnp.dot(ids.astype(jnp.float32), repeat, preferred_element_type=jnp.float32)
    own_row = jnp.where(same, (spread_ids + 0.5).astype(jnp.int32), -1)
    for at in range(0, len(relatives), 2):
        picks, gates = [], []
        for relative in relatives[at : at + 2]:
            for core in range(2):
                expert = own ^ (2 * relative + core)
                picks.append((own_row == expert).astype(jnp.float32).astype(hidden_ref.dtype))
                gates.append(
                    jnp.sum(jnp.where(ids == expert, gate_weights, 0.0), axis=1, keepdims=True)
                )
        rows = jnp.dot(
            jnp.concatenate(picks, axis=0), hidden_ref[...], preferred_element_type=jnp.float32
        )
        scaled = (rows * jnp.concatenate(gates, axis=0)).astype(hidden_ref.dtype)
        for place in range(len(picks) // 2):
            block = scaled[2 * place * token_count : 2 * (place + 1) * token_count]
            out_refs[at + place][...] = block.reshape(2, token_count, -1)


def spread_rows(hidden, expert_ids, gate_weights, own, relatives, held=None):
    token_count, choose_count, width = hidden.shape
    rows = token_count * choose_count
    vmem = pl.BlockSpec(memory_space=pltpu.VMEM)
    block = jax.ShapeDtypeStruct((2, token_count, width), hidden.dtype)
    more = [] if held is None else [held]
    scratch = [] if more else [
        pltpu.VMEM((choose_count, token_count), expert_ids.dtype),
        pltpu.VMEM((choose_count, token_count), gate_weights.dtype),
        pltpu.VMEM((rows, width), hidden.dtype),
        pltpu.SemaphoreType.DMA((3,)),
    ]
    given = vmem if more else pl.BlockSpec(memory_space=pl.ANY)
    return pl.pallas_call(
        functools.partial(spread_kernel if more else fetching_kernel, relatives),
        in_specs=[pl.BlockSpec(memory_space=pltpu.SMEM)] + [given] * 3 + [vmem] * len(more),
        out_specs=[vmem] * len(relatives),
        out_shape=[block] * len(relatives),
        scratch_shapes=scratch,
        compiler_params=pltpu.CompilerParams(vmem_limit_bytes=(24 if more else 56) << 20),
        cost_estimate=pl.CostEstimate(flops=0, bytes_accessed=0, transcendentals=0),
        name="spread_rows",
    )(
        own.reshape(1),
        expert_ids.T,
        gate_weights.T,
        hidden.reshape(rows, width),
        *more,
    )


def mix_kernel(*refs):
    rows, (near_ref, far_ref, out_ref, joined_ref) = refs[:-4], refs[-4:]
    tokens = rows[0].shape[1]

    @pl.when(pl.program_id(0) == 0)
    def _():
        for place, ref in enumerate(rows):
            joined_ref[:, place * tokens : (place + 1) * tokens] = ref[...]

    total = jnp.dot(joined_ref[0], near_ref[...], preferred_element_type=jnp.float32)
    total += jnp.dot(joined_ref[1], far_ref[...], preferred_element_type=jnp.float32)
    out_ref[...] = total.reshape(len(rows), tokens, -1).astype(out_ref.dtype)


def mix(rows, near, far, start, width, weight_of_cost):
    _, tokens, depth = rows[0].shape
    whole = pl.BlockSpec((2, tokens, depth), lambda i: (0, 0, 0))
    weight = pl.BlockSpec((depth, TILE), lambda i: (0, start // TILE + i))
    return pl.pallas_call(
        mix_kernel,
        grid=(width // TILE,),
        in_specs=[whole] * len(rows) + [weight] * 2,
        out_specs=pl.BlockSpec((len(rows), tokens, TILE), lambda i: (0, 0, i)),
        out_shape=jax.ShapeDtypeStruct((len(rows), tokens, width), jnp.bfloat16),
        scratch_shapes=[pltpu.VMEM((2, len(rows) * tokens, depth), jnp.bfloat16)],
        compiler_params=pltpu.CompilerParams(vmem_limit_bytes=24 << 20),
        cost_estimate=pl.CostEstimate(
            flops=int(weight_of_cost * 4 * len(rows) * tokens * depth * width),
            bytes_accessed=int(weight_of_cost * 4 * depth * width),
            transcendentals=0,
        ),
        name="mix",
    )(*rows, near, far)


def swap(block, axis, distance):
    return lax.ppermute(block, axis, [(i, i ^ distance) for i in range(lax.axis_size(axis))])


def send_to_chip(block, relative):
    sizes = (lax.axis_size("z"), lax.axis_size("x"))
    return lax.ppermute(
        block, ("z", "x"), [(i, i ^ relative) for i in range(sizes[0] * sizes[1])]
    )


def after(value, earlier):
    return lax.optimization_barrier((value, earlier))[0]


def dense_body(hidden, expert_ids, gate_weights, down_weight):
    own = (lax.axis_index("z") * 2 + lax.axis_index("x")) * 2 + lax.axis_index("core")
    near = down_weight[0]
    far = swap(near, "core", 1)
    odd, even = (5, 7, 1, 3), (4, 6, 0, 2)
    arrived = [None] * CHIPS
    blocks = spread_rows(hidden, expert_ids, gate_weights, own, odd)
    for relative, block in zip(odd, blocks):
        arrived[relative] = send_to_chip(block, relative)
    blocks = spread_rows(hidden, expert_ids, gate_weights, own, even, near)
    blocks = after(blocks, [arrived[r] for r in odd])
    for relative, block in zip(even, blocks):
        arrived[relative] = send_to_chip(block, relative) if relative else block
    given, kept, lines, pairs, results = [], [], [], [], []

    def mix_odd(i, earlier):
        arrived[7] = after(arrived[7], earlier)
        block = mix([arrived[r] for r in odd], near, far, *COLUMNS[i], LIGHT)
        given.append(block)
        return block

    def mix_even(parts, earlier, weight):
        start, width = COLUMNS[parts[0]][0], sum(COLUMNS[i][1] for i in parts)
        arrived[0] = after(arrived[0], earlier)
        block = mix([arrived[r] for r in even], near, far, start, width, weight)
        for i in parts:
            low = COLUMNS[i][0] - start
            kept.append(block[:, :, low : low + COLUMNS[i][1]])
        return block

    def add_x(i, earlier):
        line = after(kept[i], earlier).astype(jnp.float32) + across[i].astype(jnp.float32)
        lines.append((line[0::2], swap(line[1::2].astype(jnp.bfloat16), "z", 1)))
        return line

    def add_z(i, earlier):
        pair = after(lines[i][0], earlier) + lines[i][1].astype(jnp.float32)
        pairs.append((pair[1], swap(pair[0].astype(jnp.bfloat16), "z", 2)))
        return pair

    last = blocks[-1]
    for i in range(len(COLUMNS)):
        last = mix_odd(i, last)
    across = [swap(block, "x", 1) for block in given]
    last = mix_even((0,), last, LIGHT)
    last = add_x(0, last)
    last = mix_even((1,), last, LIGHT)
    last = mix_even((2,), last, LIGHT)
    last = add_x(1, last)
    last = add_z(0, last)
    last = add_x(2, last)
    last = add_z(1, last)
    add_z(2, last)
    for mine, theirs in pairs:
        results.append((mine + theirs.astype(jnp.float32)).astype(jnp.bfloat16))
    return jnp.concatenate(results, axis=1)


def solution(mesh):
    groups, owners, tensors = (mesh.shape[axis] for axis in ("groups", "expert", "tensor"))

    def whole(hidden, expert_ids, gate_weights, down_weight):
        tokens = hidden.shape[0] // (groups * owners)
        capacity = 2 * tokens * hidden.shape[1] // down_weight.shape[0]
        one_each = owners == 2 * CHIPS and down_weight.shape[0] == owners
        if tensors == 1 and one_each and capacity >= tokens:
            axes = ("groups", "z", "x", "core")
            used = Mesh(mesh.devices.reshape(groups, CHIPS // 2, 2, 2), axes)
            run, batch = dense_body, P(axes)
            weight, out = P(axes[1:]), P(axes)
        else:
            used, run, batch = mesh, slotted_body, P(("groups", "expert"))
            weight = P("expert", "tensor", None)
            out = P(("groups", "expert"), "tensor")
        rows = batch if tensors == 1 else P(("groups", "expert"), None, "tensor")
        return jax.shard_map(
            run,
            mesh=used,
            in_specs=(rows, batch, batch, weight),
            out_specs=out,
            check_vma=False,
        )(hidden, expert_ids, gate_weights, down_weight)

    return whole
```

```python
import functools

import jax
import jax.numpy as jnp
from jax import lax
from jax.experimental import pallas as pl
from jax.experimental.pallas import tpu as pltpu
from jax.sharding import Mesh, PartitionSpec as P

CHIPS = 8
TILE = 512
COLUMNS = ((0, 1024), (1024, 1024), (2048, 1536))
LIGHT = 0.01


def passed_along(block, axis, distance):
    devices = range(lax.axis_size(axis))
    route = [((i - distance) % len(devices), i) for i in devices]
    return lax.ppermute(block, axis, route)


def project(arrived, weights):
    return jnp.einsum("secf,efd->secd", arrived, weights, preferred_element_type=jnp.float32)


def slotted_body(hidden, expert_ids, gate_weights, down_weight):
    token_count, choose_count, half_hidden = hidden.shape
    local_experts = down_weight.shape[0]
    owner_count = lax.axis_size("expert")
    tensor_count = lax.axis_size("tensor")
    all_experts = owner_count * local_experts
    capacity = min(token_count, max(2, 2 * token_count * choose_count // all_experts))
    flat_ids = expert_ids.reshape(-1)
    onehot = (flat_ids[:, None] == jnp.arange(all_experts, dtype=jnp.int32)[None, :]).astype(
        jnp.int32
    )
    running = jnp.cumsum(onehot, axis=0)
    ranks = jnp.sum(onehot * running, axis=1) - 1
    slots = flat_ids * capacity + ranks
    copy_rows = hidden.reshape(token_count * choose_count, half_hidden)
    outgoing = (
        jnp.zeros((all_experts * capacity, half_hidden), hidden.dtype).at[slots].set(copy_rows)
    )
    outgoing = outgoing.reshape(owner_count, local_experts, capacity, half_hidden)
    width_total = down_weight.shape[2]
    width_half = width_total // tensor_count
    position = lax.axis_index("tensor")
    other = 1 - position
    arrived = lax.all_to_all(outgoing, "expert", split_axis=0, concat_axis=0, tiled=True)
    if tensor_count == 1:
        summed = project(arrived, down_weight).astype(jnp.bfloat16)
    else:
        partial_rows = project(arrived, down_weight).astype(jnp.bfloat16)
        outbound = lax.dynamic_slice_in_dim(partial_rows, other * width_half, width_half, 3)
        mine = lax.dynamic_slice_in_dim(partial_rows, position * width_half, width_half, 3)
        inbound = passed_along(outbound, "tensor", 1)
        summed = (mine.astype(jnp.float32) + inbound.astype(jnp.float32)).astype(jnp.bfloat16)
    returned = lax.all_to_all(summed, "expert", split_axis=0, concat_axis=0, tiled=True)
    flat_back = returned.reshape(all_experts * capacity, returned.shape[3])
    picked = (
        flat_back[slots].astype(jnp.float32).reshape(token_count, choose_count, returned.shape[3])
    )
    combined = jnp.sum(picked * gate_weights[:, :, None], axis=1)
    return combined.astype(jnp.bfloat16)


def fetching_kernel(relatives, own_ref, ids_hbm, gates_hbm, hidden_hbm, *refs):
    out_refs, fetched, sems = refs[: len(relatives)], refs[len(relatives) : -1], refs[-1]
    copies = [
        pltpu.make_async_copy(source, target, sems.at[i])
        for i, (source, target) in enumerate(zip((ids_hbm, gates_hbm, hidden_hbm), fetched))
    ]
    for copy in copies:
        copy.start()
    for copy in copies:
        copy.wait()
    spread_kernel(relatives, own_ref, *fetched, *out_refs)


def spread_kernel(relatives, own_ref, ids_ref, gates_ref, hidden_ref, *refs):
    out_refs = refs[-len(relatives) :]
    own = own_ref[0]
    choose_count, token_count = ids_ref.shape
    shape = (token_count, token_count * choose_count)
    row = lax.broadcasted_iota(jnp.int32, shape, 0) * choose_count
    column = lax.broadcasted_iota(jnp.int32, shape, 1)
    same = (column >= row) & (column < row + choose_count)
    across = (choose_count, token_count * choose_count)
    choice = lax.rem(lax.broadcasted_iota(jnp.int32, across, 1), choose_count)
    repeat = (choice == lax.broadcasted_iota(jnp.int32, across, 0)).astype(jnp.float32)
    ids, gate_weights = ids_ref[...].T, gates_ref[...].T
    spread_ids = jnp.dot(ids.astype(jnp.float32), repeat, preferred_element_type=jnp.float32)
    own_row = jnp.where(same, (spread_ids + 0.5).astype(jnp.int32), -1)
    for at in range(0, len(relatives), 2):
        picks, gates = [], []
        for relative in relatives[at : at + 2]:
            for core in range(2):
                expert = own ^ (2 * relative + core)
                picks.append((own_row == expert).astype(jnp.float32).astype(hidden_ref.dtype))
                gates.append(
                    jnp.sum(jnp.where(ids == expert, gate_weights, 0.0), axis=1, keepdims=True)
                )
        rows = jnp.dot(
            jnp.concatenate(picks, axis=0), hidden_ref[...], preferred_element_type=jnp.float32
        )
        scaled = (rows * jnp.concatenate(gates, axis=0)).astype(hidden_ref.dtype)
        for place in range(len(picks) // 2):
            block = scaled[2 * place * token_count : 2 * (place + 1) * token_count]
            out_refs[at + place][...] = block.reshape(2, token_count, -1)


def spread_rows(hidden, expert_ids, gate_weights, own, relatives, held=None):
    token_count, choose_count, width = hidden.shape
    rows = token_count * choose_count
    vmem = pl.BlockSpec(memory_space=pltpu.VMEM)
    block = jax.ShapeDtypeStruct((2, token_count, width), hidden.dtype)
    more = [] if held is None else [held]
    scratch = [] if more else [
        pltpu.VMEM((choose_count, token_count), expert_ids.dtype),
        pltpu.VMEM((choose_count, token_count), gate_weights.dtype),
        pltpu.VMEM((rows, width), hidden.dtype),
        pltpu.SemaphoreType.DMA((3,)),
    ]
    given = vmem if more else pl.BlockSpec(memory_space=pl.ANY)
    return pl.pallas_call(
        functools.partial(spread_kernel if more else fetching_kernel, relatives),
        in_specs=[pl.BlockSpec(memory_space=pltpu.SMEM)] + [given] * 3 + [vmem] * len(more),
        out_specs=[vmem] * len(relatives),
        out_shape=[block] * len(relatives),
        scratch_shapes=scratch,
        compiler_params=pltpu.CompilerParams(vmem_limit_bytes=(24 if more else 56) << 20),
        cost_estimate=pl.CostEstimate(flops=0, bytes_accessed=0, transcendentals=0),
        name="spread_rows",
    )(
        own.reshape(1),
        expert_ids.T,
        gate_weights.T,
        hidden.reshape(rows, width),
        *more,
    )


def mix_kernel(*refs):
    rows, (near_ref, far_ref, out_ref, joined_ref) = refs[:-4], refs[-4:]
    tokens = rows[0].shape[1]

    @pl.when(pl.program_id(0) == 0)
    def _():
        for place, ref in enumerate(rows):
            joined_ref[:, place * tokens : (place + 1) * tokens] = ref[...]

    total = jnp.dot(joined_ref[0], near_ref[...], preferred_element_type=jnp.float32)
    total += jnp.dot(joined_ref[1], far_ref[...], preferred_element_type=jnp.float32)
    out_ref[...] = total.reshape(len(rows), tokens, -1).astype(out_ref.dtype)


def mix(rows, near, far, start, width, weight_of_cost):
    _, tokens, depth = rows[0].shape
    whole = pl.BlockSpec((2, tokens, depth), lambda i: (0, 0, 0))
    weight = pl.BlockSpec((depth, TILE), lambda i: (0, start // TILE + i))
    return pl.pallas_call(
        mix_kernel,
        grid=(width // TILE,),
        in_specs=[whole] * len(rows) + [weight] * 2,
        out_specs=pl.BlockSpec((len(rows), tokens, TILE), lambda i: (0, 0, i)),
        out_shape=jax.ShapeDtypeStruct((len(rows), tokens, width), jnp.bfloat16),
        scratch_shapes=[pltpu.VMEM((2, len(rows) * tokens, depth), jnp.bfloat16)],
        compiler_params=pltpu.CompilerParams(vmem_limit_bytes=24 << 20),
        cost_estimate=pl.CostEstimate(
            flops=int(weight_of_cost * 4 * len(rows) * tokens * depth * width),
            bytes_accessed=int(weight_of_cost * 4 * depth * width),
            transcendentals=0,
        ),
        name="mix",
    )(*rows, near, far)


def swap(block, axis, distance):
    return lax.ppermute(block, axis, [(i, i ^ distance) for i in range(lax.axis_size(axis))])


def send_to_chip(block, relative):
    sizes = (lax.axis_size("z"), lax.axis_size("x"))
    return lax.ppermute(
        block, ("z", "x"), [(i, i ^ relative) for i in range(sizes[0] * sizes[1])]
    )


def after(value, earlier):
    return lax.optimization_barrier((value, earlier))[0]


def dense_body(hidden, expert_ids, gate_weights, down_weight):
    own = (lax.axis_index("z") * 2 + lax.axis_index("x")) * 2 + lax.axis_index("core")
    near = down_weight[0]
    far = swap(near, "core", 1)
    odd, even = (7, 5, 3, 1), (6, 4, 2, 0)
    arrived = [None] * CHIPS
    blocks = spread_rows(hidden, expert_ids, gate_weights, own, odd)
    for relative, block in zip(odd, blocks):
        arrived[relative] = send_to_chip(block, relative)
    blocks = spread_rows(hidden, expert_ids, gate_weights, own, even, near)
    blocks = after(blocks, [arrived[r] for r in odd])
    for relative, block in zip(even, blocks):
        arrived[relative] = send_to_chip(block, relative) if relative else block
    given, kept, lines, pairs, results = [], [], [], [], []

    def mix_odd(i, earlier):
        arrived[7] = after(arrived[7], earlier)
        block = mix([arrived[r] for r in odd], near, far, *COLUMNS[i], LIGHT)
        given.append(block)
        return block

    def mix_even(parts, earlier, weight):
        start, width = COLUMNS[parts[0]][0], sum(COLUMNS[i][1] for i in parts)
        arrived[0] = after(arrived[0], earlier)
        block = mix([arrived[r] for r in even], near, far, start, width, weight)
        for i in parts:
            low = COLUMNS[i][0] - start
            kept.append(block[:, :, low : low + COLUMNS[i][1]])
        return block

    def add_x(i, earlier):
        line = after(kept[i], earlier).astype(jnp.float32) + across[i].astype(jnp.float32)
        lines.append((line[1::2], swap(line[0::2].astype(jnp.bfloat16), "z", 1)))
        return line

    def add_z(i, earlier):
        pair = after(lines[i][0], earlier) + lines[i][1].astype(jnp.float32)
        pairs.append((pair[1], swap(pair[0].astype(jnp.bfloat16), "z", 2)))
        return pair

    last = blocks[-1]
    for i in range(len(COLUMNS)):
        last = mix_odd(i, last)
    across = [swap(block, "x", 1) for block in given]
    last = mix_even((0,), last, LIGHT)
    last = add_x(0, last)
    last = mix_even((1,), last, LIGHT)
    last = add_x(1, last)
    last = mix_even((2,), last, LIGHT)
    last = add_z(0, last)
    last = add_x(2, last)
    last = add_z(1, last)
    add_z(2, last)
    for mine, theirs in pairs:
        results.append((mine + theirs.astype(jnp.float32)).astype(jnp.bfloat16))
    return jnp.concatenate(results, axis=1)


def solution(mesh):
    groups, owners, tensors = (mesh.shape[axis] for axis in ("groups", "expert", "tensor"))

    def whole(hidden, expert_ids, gate_weights, down_weight):
        tokens = hidden.shape[0] // (groups * owners)
        capacity = 2 * tokens * hidden.shape[1] // down_weight.shape[0]
        one_each = owners == 2 * CHIPS and down_weight.shape[0] == owners
        if tensors == 1 and one_each and capacity >= tokens:
            axes = ("groups", "z", "x", "core")
            used = Mesh(mesh.devices.reshape(groups, CHIPS // 2, 2, 2), axes)
            run, batch = dense_body, P(axes)
            weight, out = P(axes[1:]), P(axes)
        else:
            used, run, batch = mesh, slotted_body, P(("groups", "expert"))
            weight = P("expert", "tensor", None)
            out = P(("groups", "expert"), "tensor")
        rows = batch if tensors == 1 else P(("groups", "expert"), None, "tensor")
        return jax.shard_map(
            run,
            mesh=used,
            in_specs=(rows, batch, batch, weight),
            out_specs=out,
            check_vma=False,
        )(hidden, expert_ids, gate_weights, down_weight)

    return whole
```
